128 devices in a mesh: gx: 16 (over z_hi, x, core), gy: 8 (over y, z_lo).
Axes of the slice: x: 4, y: 4, z: 4 (z_hi: 2, z_lo: 2; z = z_hi * 2 + z_lo), core: 2. Of those that a mesh axis runs over, the one named last changes fastest.
Arguments:
- object_field: float32 [2, 16384, 8192], P(None, 'gx', 'gy'), may hold values from -5 to 5
- probe: float32 [2, 256, 256], replicated, may hold values from -5 to 5
- centers: int32 [2048, 2], P(('gx', 'gy')), may hold values from 0 to 1023
- live: int32 [2048], P(('gx', 'gy')), may hold values from 0 to 1, as said below
- measured: float32 [2048, 256, 256], P(('gx', 'gy')), may hold values from 0.5 to 2.5
Outputs:
- object_grad: float32 [2, 16384, 8192], P(None, 'gx', 'gy')
- probe_grad: float32 [2, 256, 256], replicated
- slot_loss: float32 [2048], P(('gx', 'gy'))
The draws below stay inside these ranges and needn't reach their ends.
Inputs may be any that keep to these rules, and one draw needn't show every extreme that they name: In each tile's 16 slots the live ones come first; every tile has at least one live slot, and some tile has all 16 live.
All inputs are finite; a program needn't handle non-finite values.
Results may differ from the reference program's by a relative error of at most 0.0001.
Values sent between devices are 32-bit elements; how exact they have to be, the bound alone decides.
A program may use at most 192 MiB of HBM per device.

```python
import math
import jax
import jax.numpy as jnp
from jax import lax

M = 256
HALF = 128
TILE = 1024
PSLOT = 16
TILES = 128
SLOTS = 2048
NR = 16384
NC = 8192
N_GY = 8


def draw_live(key, part):
    counts = jax.random.randint(jax.random.fold_in(key, 11), (TILES,), 1, PSLOT + 1)
    fullest = jax.random.randint(jax.random.fold_in(key, 12), (), 0, TILES)
    counts = jnp.where(jnp.arange(TILES) == fullest, PSLOT, counts)
    slot_pos = jnp.arange(PSLOT)
    return (slot_pos[None, :] < counts[:, None]).astype(jnp.int32).reshape(SLOTS)


def set_ends(entries, own_key, least, largest):
    spot = [jax.random.randint(jax.random.fold_in(own_key, axis), (), 0, length) for axis, length in enumerate(entries.shape)]
    widest = entries.shape.index(max(entries.shape))
    next_to = spot[:widest] + [(spot[widest] + 1) % entries.shape[widest]] + spot[widest + 1:]
    return entries.at[tuple(spot)].set(least).at[tuple(next_to)].set(largest)


def steps_of(key, dims, cuts, low, largest):
    def one(position, blocks):
        heights = jax.random.uniform(jax.random.fold_in(jax.random.fold_in(key, 6), position), (blocks,), jnp.float32, low / len(cuts), largest / len(cuts))
        return jnp.repeat(jnp.exp(heights), dims[position] // blocks).reshape((-1,) + (1,) * (len(dims) - position - 1))

    level = one(*cuts[0])
    for cut in cuts[1:]:
        level = level * one(*cut)
    return level


def bell_draw(stream_key, extent, deviation, most, cuts=(), kind=jnp.bfloat16):
    result = jax.random.normal(stream_key, extent, jnp.float32) * deviation
    if len(cuts) > 0:
        result = steps_of(stream_key, extent, cuts, -0.22, 0.18) * result
    return jnp.clip(result, min=-most, max=most).astype(kind)


def setup_inputs(seed: int = 0) -> dict:
    key_of = jax.random.split(jax.random.key(seed), 6)
    object_field = bell_draw(key_of[0], (2, NR, NC), 0.7, 5.0, ((1, 16), (2, 8)), jnp.float32)
    probe = bell_draw(key_of[1], (2, M, M), 1.0, 5.0, (), jnp.float32)
    centers = set_ends(jax.random.randint(key_of[2], (SLOTS, 2), 0, TILE), jax.random.fold_in(key_of[2], 1), 0, TILE - 1).astype(jnp.int32)
    live = draw_live(jax.random.fold_in(key_of[5], 71), 0)
    measured = jnp.clip(0.5 + 2.0 * jax.random.uniform(key_of[4], (SLOTS, M, M), jnp.float32) ** steps_of(key_of[4], (SLOTS, M, M), ((0, 128),), -0.2, 0.2), 0.5, 2.5)
    return {"object_field": object_field, "probe": probe, "centers": centers, "live": live, "measured": measured}


def reference(object_field, probe, centers, live, measured):
    object_c = lax.complex(object_field[0], object_field[1])
    padded = jnp.pad(object_c, HALF)
    probe_c = lax.complex(probe[0], probe[1])
    slot_ids = jnp.arange(SLOTS, dtype=jnp.int32)
    owners = slot_ids // PSLOT
    row_start = (owners // N_GY * TILE + centers[:, 0]).astype(jnp.int32)
    col_start = (owners % N_GY * TILE + centers[:, 1]).astype(jnp.int32)

    def visit(state_now, slot_index):
        grad_pad, probe_acc = state_now
        row_at = row_start[slot_index]
        col_at = col_start[slot_index]
        patch_obj = lax.dynamic_slice(padded, (row_at, col_at), (M, M))
        farfield = jnp.fft.fft2(probe_c * patch_obj, norm='ortho')
        far_re = jnp.real(farfield)
        far_im = jnp.imag(farfield)
        modulus = jnp.sqrt(far_re * far_re + far_im * far_im + 1.0)
        differ = modulus - measured[slot_index]
        weight = live[slot_index].astype(modulus.dtype)
        adjoint = jnp.fft.ifft2(farfield * (differ / modulus * weight), norm='ortho')
        old_patch = lax.dynamic_slice(grad_pad, (row_at, col_at), (M, M))
        grad_pad = lax.dynamic_update_slice(grad_pad, old_patch + jnp.conj(probe_c) * adjoint, (row_at, col_at))
        probe_acc = probe_acc + jnp.conj(patch_obj) * adjoint
        loss = 0.5 * weight * jnp.sum(differ * differ) / (M * M)
        return ((grad_pad, probe_acc), loss)
    start = (jnp.zeros_like(padded), jnp.zeros_like(probe_c))
    (grad_pad, probe_acc), slot_loss = lax.scan(visit, start, slot_ids)
    inner = grad_pad[HALF:HALF + NR, HALF:HALF + NC]
    object_grad = jnp.stack([jnp.real(inner), jnp.imag(inner)]).astype(jnp.float32)
    probe_grad = (jnp.stack([jnp.real(probe_acc), jnp.imag(probe_acc)]) / math.sqrt(SLOTS)).astype(jnp.float32)
    return (object_grad, probe_grad, slot_loss.astype(jnp.float32))
```

```python
import functools
import math

import jax
import jax.numpy as jnp
import ml_dtypes
import numpy as np
from jax import lax
from jax.experimental import pallas as pl
from jax.experimental.pallas import tpu as pltpu
from jax.sharding import PartitionSpec as P

M = 256
HALF = 128
TILE = 1024
SLOTS_HERE = 16
ROWS = TILE + 2 * HALF
VMEM = 60 * 1024 * 1024


def split_host(table):
    high = table.astype(ml_dtypes.bfloat16)
    low = (table - high.astype(np.float64)).astype(ml_dtypes.bfloat16)
    return high, low


def host_tables():
    n = np.arange(HALF)
    lefts, rights = [], []
    for odd in (0, 1):
        k = 2 * np.arange(HALF) + odd
        angle = 2.0 * np.pi * (np.outer(k, n) % M) / M
        c, s = np.cos(angle) / 16.0, np.sin(angle) / 16.0
        both = np.block([[c, s], [-s, c]])
        for table in (both, both.T):
            high, low = split_host(table)
            lefts.append(np.concatenate([high, low, high], axis=1))
            rights.append(np.concatenate([high, high, low], axis=0))
    pick = np.zeros((M, M))
    pick[2 * n, n] = 1.0
    pick[2 * n + 1, HALF + n] = 1.0
    pick = pick.astype(ml_dtypes.bfloat16)
    return np.stack(lefts), np.stack(rights), np.concatenate([pick, pick], axis=0)


def halves(x):
    high = x.astype(jnp.bfloat16)
    low = (x - high.astype(jnp.float32)).astype(jnp.bfloat16)
    return high, low


def left_product(table, x):
    high, low = halves(x)
    return jnp.dot(table, jnp.concatenate([high, high, low], axis=0), preferred_element_type=jnp.float32)


def right_product(x, table):
    high, low = halves(x)
    return jnp.dot(jnp.concatenate([high, low, high], axis=1), table, preferred_element_type=jnp.float32)


def visit(obj, grad, probe, seen, slot, lefts, rights, pick, acc, row, block, block_end, shift):
    lane = lax.broadcasted_iota(jnp.int32, (M, HALF), 1)
    wraps = lane < shift
    rows = pl.ds(row, M)

    def window(part):
        first = jnp.where(wraps, obj[part, block_end, rows, :], obj[part, block, rows, :])
        return jnp.concatenate([first, obj[part, block + 1, rows, :]], axis=1)

    obj_re, obj_im = window(0), window(1)
    probe_re = pltpu.roll(probe[0], shift, 1)
    probe_im = pltpu.roll(probe[1], shift, 1)
    wave_re = probe_re * obj_re - probe_im * obj_im
    wave_im = probe_re * obj_im + probe_im * obj_re
    top, low = slice(0, HALF), slice(HALF, M)
    even = left_product(lefts[0], jnp.concatenate([wave_re[top] + wave_re[low], wave_im[top] + wave_im[low]], axis=0))
    odd = left_product(lefts[2], jnp.concatenate([wave_re[top] - wave_re[low], wave_im[top] - wave_im[low]], axis=0))
    half_re = jnp.concatenate([even[top], odd[top]], axis=0)
    half_im = jnp.concatenate([even[low], odd[low]], axis=0)
    far_e = right_product(
        jnp.concatenate([half_re[:, top] + half_re[:, low], half_im[:, top] + half_im[:, low]], axis=1), rights[1]
    )
    far_o = right_product(
        jnp.concatenate([half_re[:, top] - half_re[:, low], half_im[:, top] - half_im[:, low]], axis=1), rights[3]
    )
    meas = jnp.concatenate(
        [
            jnp.concatenate([seen[slot, side, pl.ds(odd, HALF, stride=2), :] for side in range(2)], axis=1)
            for odd in range(2)
        ],
        axis=0,
    )
    meas = jnp.dot(jnp.concatenate(halves(meas), axis=1), pick[...], preferred_element_type=jnp.float32)

    def residual(far, seen):
        squares = far * far
        total = squares[:, top] + squares[:, low] + 1.0
        inverse = lax.rsqrt(total)
        differ = total * inverse - seen
        factor = differ * inverse
        return far * jnp.concatenate([factor, factor], axis=1), differ * differ

    back_e, loss_e = residual(far_e, meas[:, top])
    back_o, loss_o = residual(far_o, meas[:, low])
    loss = jnp.sum(loss_e + loss_o) * (0.5 / (M * M))
    up = right_product(back_e, rights[0])
    vp = right_product(back_o, rights[2])
    plus, minus = up + vp, up - vp
    half_re = jnp.concatenate([plus[:, top], minus[:, top]], axis=1)
    half_im = jnp.concatenate([plus[:, low], minus[:, low]], axis=1)
    up = left_product(lefts[1], jnp.concatenate([half_re[top], half_im[top]], axis=0))
    vp = left_product(lefts[3], jnp.concatenate([half_re[low], half_im[low]], axis=0))
    plus, minus = up + vp, up - vp
    back_re = jnp.concatenate([plus[top], minus[top]], axis=0)
    back_im = jnp.concatenate([plus[low], minus[low]], axis=0)

    grads = (probe_re * back_re + probe_im * back_im, probe_re * back_im - probe_im * back_re)
    for part, g in enumerate(grads):
        first = g[:, top]
        grad[part, block, rows, :] += jnp.where(wraps, 0.0, first)
        grad[part, block + 1, rows, :] += g[:, low]
        grad[part, block_end, rows, :] += jnp.where(wraps, first, 0.0)
    unshift = lax.rem(M - shift, M)
    terms = (obj_re * back_re + obj_im * back_im, obj_re * back_im - obj_im * back_re)
    for part, term in enumerate(terms):
        turned = pltpu.roll(term, unshift, 1)
        acc[part, 0] += turned[:, top]
        acc[part, 1] += turned[:, low]
    return loss


EDGE = slice(HALF, HALF + TILE)
STRIP = (0, 1, 6, 7)
CORE = TILE - 2 * HALF


def start_all(pairs, sems):
    copies = [pltpu.make_async_copy(source, target, sems.at[i]) for i, (source, target) in enumerate(pairs)]
    for copy in copies:
        copy.start()
    return copies


def wait_all(copies):
    for copy in copies:
        copy.wait()


def block_of(ref, index):
    return ref.at[:, :, pl.ds(HALF * index, HALF)]


def tile_pairs(tile, up, down, buffer, slots):
    pairs = []
    for place, block in slots:
        pairs.append((block_of(tile, block), buffer.at[:, place, pl.ds(HALF, TILE)]))
        pairs.append((block_of(up, block), buffer.at[:, place, pl.ds(0, HALF)]))
        pairs.append((block_of(down, block), buffer.at[:, place, pl.ds(HALF + TILE, HALF)]))
    return pairs


def side_pairs(edge, core, above, below, side, buffer, place):
    return [
        (edge.at[:, pl.ds(0, HALF)], buffer.at[:, place, pl.ds(HALF, HALF)]),
        (core, buffer.at[:, place, pl.ds(2 * HALF, CORE)]),
        (edge.at[:, pl.ds(HALF, HALF)], buffer.at[:, place, pl.ds(TILE, HALF)]),
        (block_of(above, side), buffer.at[:, place, pl.ds(0, HALF)]),
        (block_of(below, side), buffer.at[:, place, pl.ds(HALF + TILE, HALF)]),
    ]


def flipped(pairs):
    return [(target, source) for source, target in pairs]


def slot_copies(measured, seen, slot_sems, s):
    return [
        pltpu.make_async_copy(measured.at[s, :, pl.ds(HALF * side, HALF)], seen.at[s, side], slot_sems.at[s, side])
        for side in range(2)
    ]


def fetch_slots(live, centers, wanted, measured, seen, slot_sems):
    def fetch(s, carry):
        @pl.when(wanted(live[s], centers[s, 1]))
        def _():
            for copy in slot_copies(measured, seen, slot_sems, s):
                copy.start()

        return carry

    lax.fori_loop(0, SLOTS_HERE, fetch, 0)


def run_slots(live, centers, wanted, place, measured, seen, slot_sems, losses, body):
    def step(s, carry):
        column = centers[s, 1]

        @pl.when(wanted(live[s], column))
        def _():
            wait_all(slot_copies(measured, seen, slot_sems, s))
            block, block_end, shift = place(column)
            losses[s] = body(s, centers[s, 0], block, block_end, shift)

        return carry

    lax.fori_loop(0, SLOTS_HERE, step, 0)


def is_inner(alive, column):
    return (alive > 0) & (column >= HALF) & (column <= TILE - HALF)


def is_outer(alive, column):
    return (alive > 0) & ((column < HALF) | (column > TILE - HALF))


def inner_kernel(
    centers, live, probe, lefts, rights, pick, field, up, down, measured,
    grad_out, up_out, down_out, acc, losses, obj, grad, seen, sems, slot_sems,
):
    slots = [(j, j) for j in range(8)]
    loads = start_all(tile_pairs(field, up, down, obj, slots), sems)
    fetch_slots(live, centers, is_inner, measured, seen, slot_sems)
    grad[...] = jnp.zeros_like(grad)
    acc[...] = jnp.zeros_like(acc)
    for s in range(SLOTS_HERE):
        losses[s] = 0.0
    wait_all(loads)

    def place(column):
        start = column - HALF
        block = lax.div(start, HALF)
        return block, jnp.minimum(block + 2, 7), lax.rem(start, HALF)

    def body(s, row, block, block_end, shift):
        return visit(obj, grad, probe, seen, s, lefts, rights, pick, acc, row, block, block_end, shift)

    run_slots(live, centers, is_inner, place, measured, seen, slot_sems, losses, body)
    wait_all(start_all(flipped(tile_pairs(grad_out, up_out, down_out, grad, slots)), sems))


def outer_kernel(
    centers, live, probe, lefts, rights, pick, field, up, down, measured,
    left_edge, left_core, right_edge, right_core, above, below, grad_in, up_in, down_in, acc_in, losses_in,
    grad_out, up_out, down_out, acc, losses, gleft_edge, gleft_core, gright_edge, gright_core, gabove, gbelow,
    obj, grad, seen, sems, slot_sems,
):
    slots = list(zip((1, 2, 3, 4), STRIP))
    loads = start_all(
        tile_pairs(field, up, down, obj, slots)
        + side_pairs(left_edge, left_core, above, below, 0, obj, 0)
        + side_pairs(right_edge, right_core, above, below, 1, obj, 5)
        + tile_pairs(grad_in, up_in, down_in, grad, slots),
        sems,
    )
    fetch_slots(live, centers, is_outer, measured, seen, slot_sems)
    for place_at in (0, 5):
        grad[:, place_at] = jnp.zeros((2, ROWS, HALF), jnp.float32)
    acc[...] = acc_in[...]
    for s in range(SLOTS_HERE):
        losses[s] = losses_in[s]
    wait_all(loads)

    def place(column):
        at_left = column < HALF
        block = jnp.where(at_left, 0, 3)
        return block, block + 2, jnp.where(at_left, column, column - (TILE - HALF))

    def body(s, row, block, block_end, shift):
        return visit(obj, grad, probe, seen, s, lefts, rights, pick, acc, row, block, block_end, shift)

    run_slots(live, centers, is_outer, place, measured, seen, slot_sems, losses, body)
    wait_all(
        start_all(
            flipped(
                tile_pairs(grad_out, up_out, down_out, grad, slots)
                + side_pairs(gleft_edge, gleft_core, gabove, gbelow, 0, grad, 0)
                + side_pairs(gright_edge, gright_core, gabove, gbelow, 1, grad, 5)
            ),
            sems,
        )
    )


VMEM_SPEC = pl.BlockSpec(memory_space=pltpu.VMEM)
SMEM_SPEC = pl.BlockSpec(memory_space=pltpu.SMEM)
HBM_SPEC = pl.BlockSpec(memory_space=pl.ANY)


def shaped(*shape):
    return jax.ShapeDtypeStruct(shape, jnp.float32)


def slot_scratch(blocks, copies):
    return [
        pltpu.VMEM((2, blocks, ROWS, HALF), jnp.float32),
        pltpu.VMEM((2, blocks, ROWS, HALF), jnp.float32),
        pltpu.VMEM((SLOTS_HERE, 2, M, HALF), jnp.float32),
        pltpu.SemaphoreType.DMA((copies,)),
        pltpu.SemaphoreType.DMA((SLOTS_HERE, 2)),
    ]


def cost(slots):
    return pl.CostEstimate(flops=slots * 26 * 2 * M**3, bytes_accessed=30 << 20, transcendentals=slots * M * M)


TILE_OUT = (shaped(2, TILE, TILE), shaped(2, HALF, TILE), shaped(2, HALF, TILE), shaped(2, 2, M, HALF), shaped(SLOTS_HERE))


def inner_slots(centers, live, probe, tables, field, up, down, measured):
    return pl.pallas_call(
        inner_kernel,
        out_shape=TILE_OUT,
        in_specs=[SMEM_SPEC] * 2 + [VMEM_SPEC] * 4 + [HBM_SPEC] * 4,
        out_specs=(HBM_SPEC, HBM_SPEC, HBM_SPEC, VMEM_SPEC, SMEM_SPEC),
        scratch_shapes=slot_scratch(8, 24),
        compiler_params=pltpu.CompilerParams(vmem_limit_bytes=VMEM),
        cost_estimate=cost(SLOTS_HERE),
        name="inner_slots",
    )(centers, live, probe, *tables, field, up, down, measured)


def outer_slots(centers, live, probe, tables, field, up, down, measured, halos, partial):
    return pl.pallas_call(
        outer_kernel,
        out_shape=TILE_OUT
        + (shaped(2, 2 * HALF, HALF), shaped(2, CORE, HALF)) * 2
        + (shaped(2, HALF, 2 * HALF),) * 2,
        in_specs=[SMEM_SPEC] * 2 + [VMEM_SPEC] * 4 + [HBM_SPEC] * 4 + [HBM_SPEC] * 9 + [VMEM_SPEC, SMEM_SPEC],
        out_specs=(HBM_SPEC, HBM_SPEC, HBM_SPEC, VMEM_SPEC, SMEM_SPEC) + (HBM_SPEC,) * 6,
        scratch_shapes=slot_scratch(6, 34),
        input_output_aliases={16: 0, 17: 1, 18: 2},
        compiler_params=pltpu.CompilerParams(vmem_limit_bytes=VMEM),
        cost_estimate=cost(SLOTS_HERE // 2),
        name="outer_slots",
    )(centers, live, probe, *tables, field, up, down, measured, *halos, *partial)


def fold_kernel(pieces, *refs):
    sources, (tile, out), (have, got, sems) = refs[: len(pieces)], refs[len(pieces) : len(pieces) + 2], refs[len(pieces) + 2 :]
    pairs, targets = [], []
    for source, (take, at, size, lanes, width, base) in zip(sources, pieces):
        pairs.append((source.at[:, pl.ds(take, size)], got.at[:, pl.ds(base, size)]))
        pairs.append((tile.at[:, pl.ds(at, size), pl.ds(lanes, width)], have.at[:, pl.ds(base, size)]))
        targets.append((have.at[:, pl.ds(base, size)], out.at[:, pl.ds(at, size), pl.ds(lanes, width)]))
    wait_all(start_all(pairs, sems))
    have[...] += got[...]
    wait_all(start_all(targets, sems))


def fold(tile, sources, pieces, rows, width):
    n = len(pieces)
    return pl.pallas_call(
        functools.partial(fold_kernel, pieces),
        out_shape=shaped(2, TILE, TILE),
        in_specs=[HBM_SPEC] * (n + 1),
        out_specs=HBM_SPEC,
        scratch_shapes=[
            pltpu.VMEM((2, rows, width), jnp.float32),
            pltpu.VMEM((2, rows, width), jnp.float32),
            pltpu.SemaphoreType.DMA((2 * n,)),
        ],
        input_output_aliases={n: 0},
        compiler_params=pltpu.CompilerParams(vmem_limit_bytes=VMEM),
        cost_estimate=pl.CostEstimate(flops=2 * rows * width, bytes_accessed=24 * rows * width, transcendentals=0),
        name="fold",
    )(*sources, tile)


MESH = pl.DeviceIdType.MESH
SHARE = 8


def sum_kernel(scale, part, out, first, second, third, kept1, kept2, kept3, full, send_sems, recv_sems):
    gx, gy = lax.axis_index("gx"), lax.axis_index("gy")
    core = lax.rem(gx, 2)
    spot = lax.rem(lax.div(gx, 2), 4)
    upper = lax.div(gx, 8)
    group = upper * 8 + gy

    def at_core(k):
        return (gx - core + k, gy)

    def at_spot(k):
        return (gx + 2 * (k - spot), gy)

    def at_group(k):
        return (gx + 8 * (lax.div(k, 8) - upper), lax.rem(k, 8))

    other = at_core(1 - core)
    spots = [lax.rem(spot + d, 4) for d in range(1, 4)]
    groups = [lax.rem(group + d, 16) for d in range(1, 16)]
    barrier = pltpu.get_barrier_semaphore()
    partners = [other] + [at_spot(k) for k in spots] + [at_group(k) for k in groups]
    for device in partners:
        pl.semaphore_signal(barrier, inc=1, device_id=device, device_id_type=MESH)
    pl.semaphore_wait(barrier, len(partners))

    def rows(start, size):
        return pl.ds(pl.multiple_of(start, 8), size)

    count = [0]

    def send(source, target, device):
        i = count[0]
        count[0] += 1
        copy = pltpu.make_async_remote_copy(
            src_ref=source, dst_ref=target, send_sem=send_sems.at[i], recv_sem=recv_sems.at[i],
            device_id=device, device_id_type=MESH,
        )
        copy.start()
        return copy

    def exchange(copies):
        for copy in copies:
            copy.wait_recv()
        return copies

    sent = exchange([send(part.at[rows((1 - core) * 512, 512)], first, other)])
    kept1[...] = part[rows(core * 512, 512), :] + first[...]
    sent += exchange(
        [send(kept1.at[rows(k * 128, 128)], second.at[d], at_spot(k)) for d, k in enumerate(spots)]
    )
    kept2[...] = kept1[rows(spot * 128, 128), :] + (second[0] + second[1] + second[2])
    sent += exchange(
        [send(kept2.at[rows(k * SHARE, SHARE)], third.at[d], at_group(k)) for d, k in enumerate(groups)]
    )
    total = kept2[rows(group * SHARE, SHARE), :]
    for d in range(15):
        total = total + third[d]
    kept3[...] = total * scale
    mine = rows(core * 512 + spot * 128 + group * SHARE, SHARE)
    full[mine, :] = kept3[...]
    sent += exchange([send(kept3, full.at[mine], at_group(k)) for k in groups])
    quarter = full.at[rows(core * 512 + spot * 128, 128)]
    sent += exchange([send(quarter, quarter, at_spot(k)) for k in spots])
    whole = full.at[rows(core * 512, 512)]
    sent += exchange([send(whole, whole, other)])
    for part_at in range(2):
        for side in range(2):
            out[part_at, :, HALF * side : HALF * (side + 1)] = full[pl.ds((part_at * 2 + side) * M, M), :]
    for copy in sent:
        copy.wait_send()


def sum_everywhere(part, scale):
    copies = 2 * (1 + 3 + 15)
    return pl.pallas_call(
        functools.partial(sum_kernel, scale),
        out_shape=shaped(2, M, M),
        in_specs=[VMEM_SPEC],
        out_specs=VMEM_SPEC,
        scratch_shapes=[
            pltpu.VMEM((512, HALF), jnp.float32),
            pltpu.VMEM((3, 128, HALF), jnp.float32),
            pltpu.VMEM((15, SHARE, HALF), jnp.float32),
            pltpu.VMEM((512, HALF), jnp.float32),
            pltpu.VMEM((128, HALF), jnp.float32),
            pltpu.VMEM((SHARE, HALF), jnp.float32),
            pltpu.VMEM((1024, HALF), jnp.float32),
            pltpu.SemaphoreType.DMA((copies,)),
            pltpu.SemaphoreType.DMA((copies,)),
        ],
        compiler_params=pltpu.CompilerParams(collective_id=0, has_side_effects=True),
        cost_estimate=pl.CostEstimate(flops=M * M * 8, bytes_accessed=16 << 20, transcendentals=0),
        name="sum_everywhere",
    )(part.reshape(1024, HALF))


def shift_by_one(x, axis, forward):
    count = lax.axis_size(axis)
    steps = [(i, i + 1) if forward else (i + 1, i) for i in range(count - 1)]
    return lax.ppermute(x, axis, steps)


def to_right(x):
    return shift_by_one(x, "gy", True)


def to_left(x):
    return shift_by_one(x, "gy", False)


def to_down(x):
    return shift_by_one(x, "gx", True)


def to_up(x):
    return shift_by_one(x, "gx", False)


def ends(strip):
    return jnp.concatenate([strip[:, :HALF], strip[:, TILE - HALF :]], axis=1)


def on_device(field, probe, centers, live, measured):
    tables = tuple(jnp.asarray(t) for t in host_tables())
    first, last = field[:, :, :HALF], field[:, :, TILE - HALF :]
    left_edge, right_edge = to_right(ends(last)), to_left(ends(first))
    left_core, right_core = to_right(last[:, HALF : TILE - HALF]), to_left(first[:, HALF : TILE - HALF])
    up, down = to_down(field[:, TILE - HALF :]), to_up(field[:, :HALF])
    above = to_down(jnp.concatenate([left_edge[:, HALF:], right_edge[:, HALF:]], axis=2))
    below = to_up(jnp.concatenate([left_edge[:, :HALF], right_edge[:, :HALF]], axis=2))
    halos = (left_edge, left_core, right_edge, right_core, above, below)
    partial = inner_slots(centers, live, probe, tables, field, up, down, measured)
    grad, gup, gdown, acc, losses, gle, glc, gre, grc, gabove, gbelow = outer_slots(
        centers, live, probe, tables, field, up, down, measured, halos, partial
    )
    from_right_core, from_left_core = to_left(glc), to_right(grc)
    from_down, from_up = to_up(gabove), to_down(gbelow)
    more_left = jnp.concatenate([from_up[:, :, :HALF], from_down[:, :, :HALF]], axis=1)
    more_right = jnp.concatenate([from_up[:, :, HALF:], from_down[:, :, HALF:]], axis=1)
    from_right_edge, from_left_edge = to_left(gle + more_left), to_right(gre + more_right)
    row_down, row_up = to_up(gup), to_down(gdown)
    slots_all = SLOTS_HERE * lax.axis_size("gx") * lax.axis_size("gy")
    probe_grad = sum_everywhere(acc, 1.0 / math.sqrt(slots_all))
    end = TILE - HALF
    grad = fold(
        grad, (row_up, row_down), ((0, 0, HALF, 0, TILE, 0), (0, end, HALF, 0, TILE, HALF)), 2 * HALF, TILE
    )
    grad = fold(
        grad,
        (from_left_edge, from_left_core, from_left_edge, from_right_edge, from_right_core, from_right_edge),
        (
            (0, 0, HALF, 0, HALF, 0),
            (0, HALF, CORE, 0, HALF, HALF),
            (HALF, end, HALF, 0, HALF, end),
            (0, 0, HALF, end, HALF, TILE),
            (0, HALF, CORE, end, HALF, TILE + HALF),
            (HALF, end, HALF, end, HALF, TILE + end),
        ),
        2 * TILE,
        HALF,
    )
    return grad, probe_grad, losses


def solution(mesh):
    placed = (
        P(None, "gx", "gy"),
        P(),
        P(("gx", "gy"), None),
        P(("gx", "gy")),
        P(("gx", "gy"), None, None),
    )
    return jax.shard_map(
        on_device,
        mesh=mesh,
        in_specs=placed,
        out_specs=(P(None, "gx", "gy"), P(), P(("gx", "gy"))),
        check_vma=False,
    )
```

```python
import functools
import math

import jax
import jax.numpy as jnp
import ml_dtypes
import numpy as np
from jax import lax
from jax.experimental import pallas as pl
from jax.experimental.pallas import tpu as pltpu
from jax.sharding import PartitionSpec as P

M = 256
HALF = 128
TILE = 1024
SLOTS_HERE = 16
ROWS = TILE + 2 * HALF
VMEM = 60 * 1024 * 1024


def split_host(table):
    high = table.astype(ml_dtypes.bfloat16)
    low = (table - high.astype(np.float64)).astype(ml_dtypes.bfloat16)
    return high, low


def host_tables():
    n = np.arange(HALF)
    lefts, rights = [], []
    for odd in (0, 1):
        k = 2 * np.arange(HALF) + odd
        angle = 2.0 * np.pi * (np.outer(k, n) % M) / M
        c, s = np.cos(angle) / 16.0, np.sin(angle) / 16.0
        both = np.block([[c, s], [-s, c]])
        for table in (both, both.T):
            high, low = split_host(table)
            lefts.append(np.concatenate([high, low, high], axis=1))
            rights.append(np.concatenate([high, high, low], axis=0))
    pick = np.zeros((M, M))
    pick[2 * n, n] = 1.0
    pick[2 * n + 1, HALF + n] = 1.0
    pick = pick.astype(ml_dtypes.bfloat16)
    return np.stack(lefts), np.stack(rights), np.concatenate([pick, pick], axis=0)


def halves(x):
    high = x.astype(jnp.bfloat16)
    low = (x - high.astype(jnp.float32)).astype(jnp.bfloat16)
    return high, low


def left_product(table, x):
    high, low = halves(x)
    return jnp.dot(table, jnp.concatenate([high, high, low], axis=0), preferred_element_type=jnp.float32)


def right_product(x, table):
    high, low = halves(x)
    return jnp.dot(jnp.concatenate([high, low, high], axis=1), table, preferred_element_type=jnp.float32)


def visit(obj, grad, probe, seen, slot, lefts, rights, pick, acc, row, block, block_end, shift):
    lane = lax.broadcasted_iota(jnp.int32, (M, HALF), 1)
    wraps = lane < shift
    rows = pl.ds(row, M)

    def window(part):
        first = jnp.where(wraps, obj[part, block_end, rows, :], obj[part, block, rows, :])
        return jnp.concatenate([first, obj[part, block + 1, rows, :]], axis=1)

    obj_re, obj_im = window(0), window(1)
    probe_re = pltpu.roll(probe[0], shift, 1)
    probe_im = pltpu.roll(probe[1], shift, 1)
    wave_re = probe_re * obj_re - probe_im * obj_im
    wave_im = probe_re * obj_im + probe_im * obj_re
    top, low = slice(0, HALF), slice(HALF, M)
    even = left_product(lefts[0], jnp.concatenate([wave_re[top] + wave_re[low], wave_im[top] + wave_im[low]], axis=0))
    odd = left_product(lefts[2], jnp.concatenate([wave_re[top] - wave_re[low], wave_im[top] - wave_im[low]], axis=0))
    half_re = jnp.concatenate([even[top], odd[top]], axis=0)
    half_im = jnp.concatenate([even[low], odd[low]], axis=0)
    far_e = right_product(
        jnp.concatenate([half_re[:, top] + half_re[:, low], half_im[:, top] + half_im[:, low]], axis=1), rights[1]
    )
    far_o = right_product(
        jnp.concatenate([half_re[:, top] - half_re[:, low], half_im[:, top] - half_im[:, low]], axis=1), rights[3]
    )
    meas = jnp.concatenate(
        [
            jnp.concatenate([seen[slot, side, pl.ds(odd, HALF, stride=2), :] for side in range(2)], axis=1)
            for odd in range(2)
        ],
        axis=0,
    )
    meas = jnp.dot(jnp.concatenate(halves(meas), axis=1), pick[...], preferred_element_type=jnp.float32)

    def residual(far, seen):
        squares = far * far
        total = squares[:, top] + squares[:, low] + 1.0
        inverse = lax.rsqrt(total)
        differ = total * inverse - seen
        factor = differ * inverse
        return far * jnp.concatenate([factor, factor], axis=1), differ * differ

    back_e, loss_e = residual(far_e, meas[:, top])
    back_o, loss_o = residual(far_o, meas[:, low])
    loss = jnp.sum(loss_e + loss_o) * (0.5 / (M * M))
    up = right_product(back_e, rights[0])
    vp = right_product(back_o, rights[2])
    plus, minus = up + vp, up - vp
    half_re = jnp.concatenate([plus[:, top], minus[:, top]], axis=1)
    half_im = jnp.concatenate([plus[:, low], minus[:, low]], axis=1)
    up = left_product(lefts[1], jnp.concatenate([half_re[top], half_im[top]], axis=0))
    vp = left_product(lefts[3], jnp.concatenate([half_re[low], half_im[low]], axis=0))
    plus, minus = up + vp, up - vp
    back_re = jnp.concatenate([plus[top], minus[top]], axis=0)
    back_im = jnp.concatenate([plus[low], minus[low]], axis=0)

    grads = (probe_re * back_re + probe_im * back_im, probe_re * back_im - probe_im * back_re)
    for part, g in enumerate(grads):
        first = g[:, top]
        grad[part, block, rows, :] += jnp.where(wraps, 0.0, first)
        grad[part, block + 1, rows, :] += g[:, low]
        grad[part, block_end, rows, :] += jnp.where(wraps, first, 0.0)
    unshift = lax.rem(M - shift, M)
    terms = (obj_re * back_re + obj_im * back_im, obj_re * back_im - obj_im * back_re)
    for part, term in enumerate(terms):
        turned = pltpu.roll(term, unshift, 1)
        acc[part, 0] += turned[:, top]
        acc[part, 1] += turned[:, low]
    return loss


EDGE = slice(HALF, HALF + TILE)
STRIP = (0, 1, 6, 7)
CORE = TILE - 2 * HALF


def start_all(pairs, sems):
    copies = [pltpu.make_async_copy(source, target, sems.at[i]) for i, (source, target) in enumerate(pairs)]
    for copy in copies:
        copy.start()
    return copies


def wait_all(copies):
    for copy in copies:
        copy.wait()


def block_of(ref, index):
    return ref.at[:, :, pl.ds(HALF * index, HALF)]


def tile_pairs(tile, up, down, buffer, slots):
    pairs = []
    for place, block in slots:
        pairs.append((block_of(tile, block), buffer.at[:, place, pl.ds(HALF, TILE)]))
        pairs.append((block_of(up, block), buffer.at[:, place, pl.ds(0, HALF)]))
        pairs.append((block_of(down, block), buffer.at[:, place, pl.ds(HALF + TILE, HALF)]))
    return pairs


def halo_pairs(edge, core, above, below, side, buffer, place):
    return [
        (edge.at[:, pl.ds(0, HALF)], buffer.at[:, place, pl.ds(HALF, HALF)]),
        (core, buffer.at[:, place, pl.ds(2 * HALF, CORE)]),
        (edge.at[:, pl.ds(HALF, HALF)], buffer.at[:, place, pl.ds(TILE, HALF)]),
        (block_of(above, side), buffer.at[:, place, pl.ds(0, HALF)]),
        (block_of(below, side), buffer.at[:, place, pl.ds(HALF + TILE, HALF)]),
    ]


def strip_pairs(strip, above, below, side, buffer, place):
    return [
        (strip, buffer.at[:, place, pl.ds(HALF, TILE)]),
        (block_of(above, side), buffer.at[:, place, pl.ds(0, HALF)]),
        (block_of(below, side), buffer.at[:, place, pl.ds(HALF + TILE, HALF)]),
    ]


def flipped(pairs):
    return [(target, source) for source, target in pairs]


def slot_copies(measured, seen, slot_sems, s):
    return [
        pltpu.make_async_copy(measured.at[s, :, pl.ds(HALF * side, HALF)], seen.at[s, side], slot_sems.at[s, side])
        for side in range(2)
    ]


def fetch_slots(live, centers, wanted, measured, seen, slot_sems):
    def fetch(s, carry):
        @pl.when(wanted(live[s], centers[s, 1]))
        def _():
            for copy in slot_copies(measured, seen, slot_sems, s):
                copy.start()

        return carry

    lax.fori_loop(0, SLOTS_HERE, fetch, 0)


def run_slots(live, centers, wanted, place, measured, seen, slot_sems, losses, body):
    def step(s, carry):
        column = centers[s, 1]

        @pl.when(wanted(live[s], column))
        def _():
            wait_all(slot_copies(measured, seen, slot_sems, s))
            block, block_end, shift = place(column)
            losses[s] = body(s, centers[s, 0], block, block_end, shift)

        return carry

    lax.fori_loop(0, SLOTS_HERE, step, 0)


def is_inner(alive, column):
    return (alive > 0) & (column >= HALF) & (column <= TILE - HALF)


def is_outer(alive, column):
    return (alive > 0) & ((column < HALF) | (column > TILE - HALF))


def inner_kernel(
    centers, live, probe, lefts, rights, pick, field, up, down, measured,
    grad_out, up_out, down_out, acc, losses, obj, grad, seen, sems, slot_sems,
):
    slots = [(j, j) for j in range(8)]
    loads = start_all(tile_pairs(field, up, down, obj, slots), sems)
    fetch_slots(live, centers, is_inner, measured, seen, slot_sems)
    grad[...] = jnp.zeros_like(grad)
    acc[...] = jnp.zeros_like(acc)
    for s in range(SLOTS_HERE):
        losses[s] = 0.0
    wait_all(loads)

    def place(column):
        start = column - HALF
        block = lax.div(start, HALF)
        return block, jnp.minimum(block + 2, 7), lax.rem(start, HALF)

    def body(s, row, block, block_end, shift):
        return visit(obj, grad, probe, seen, s, lefts, rights, pick, acc, row, block, block_end, shift)

    run_slots(live, centers, is_inner, place, measured, seen, slot_sems, losses, body)
    wait_all(start_all(flipped(tile_pairs(grad_out, up_out, down_out, grad, slots)), sems))


def outer_kernel(
    centers, live, probe, lefts, rights, pick, field, up, down, measured,
    left_edge, left_core, right_edge, right_core, above, below, grad_in, up_in, down_in, acc_in, losses_in,
    grad_out, up_out, down_out, acc, losses, gleft, gright, gabove, gbelow,
    obj, grad, seen, sems, slot_sems,
):
    slots = list(zip((1, 2, 3, 4), STRIP))
    loads = start_all(
        tile_pairs(field, up, down, obj, slots)
        + halo_pairs(left_edge, left_core, above, below, 0, obj, 0)
        + halo_pairs(right_edge, right_core, above, below, 1, obj, 5)
        + tile_pairs(grad_in, up_in, down_in, grad, slots),
        sems,
    )
    fetch_slots(live, centers, is_outer, measured, seen, slot_sems)
    for place_at in (0, 5):
        grad[:, place_at] = jnp.zeros((2, ROWS, HALF), jnp.float32)
    acc[...] = acc_in[...]
    for s in range(SLOTS_HERE):
        losses[s] = losses_in[s]
    wait_all(loads)

    def place(column):
        at_left = column < HALF
        block = jnp.where(at_left, 0, 3)
        return block, block + 2, jnp.where(at_left, column, column - (TILE - HALF))

    def body(s, row, block, block_end, shift):
        return visit(obj, grad, probe, seen, s, lefts, rights, pick, acc, row, block, block_end, shift)

    run_slots(live, centers, is_outer, place, measured, seen, slot_sems, losses, body)
    wait_all(
        start_all(
            flipped(
                tile_pairs(grad_out, up_out, down_out, grad, slots)
                + strip_pairs(gleft, gabove, gbelow, 0, grad, 0)
                + strip_pairs(gright, gabove, gbelow, 1, grad, 5)
            ),
            sems,
        )
    )


VMEM_SPEC = pl.BlockSpec(memory_space=pltpu.VMEM)
SMEM_SPEC = pl.BlockSpec(memory_space=pltpu.SMEM)
HBM_SPEC = pl.BlockSpec(memory_space=pl.ANY)


def shaped(*shape):
    return jax.ShapeDtypeStruct(shape, jnp.float32)


def slot_scratch(blocks, copies):
    return [
        pltpu.VMEM((2, blocks, ROWS, HALF), jnp.float32),
        pltpu.VMEM((2, blocks, ROWS, HALF), jnp.float32),
        pltpu.VMEM((SLOTS_HERE, 2, M, HALF), jnp.float32),
        pltpu.SemaphoreType.DMA((copies,)),
        pltpu.SemaphoreType.DMA((SLOTS_HERE, 2)),
    ]


def cost(slots):
    return pl.CostEstimate(flops=slots * 26 * 2 * M**3, bytes_accessed=30 << 20, transcendentals=slots * M * M)


TILE_OUT = (shaped(2, TILE, TILE), shaped(2, HALF, TILE), shaped(2, HALF, TILE), shaped(2, 2, M, HALF), shaped(SLOTS_HERE))


def inner_slots(centers, live, probe, tables, field, up, down, measured):
    return pl.pallas_call(
        inner_kernel,
        out_shape=TILE_OUT,
        in_specs=[SMEM_SPEC] * 2 + [VMEM_SPEC] * 4 + [HBM_SPEC] * 4,
        out_specs=(HBM_SPEC, HBM_SPEC, HBM_SPEC, VMEM_SPEC, SMEM_SPEC),
        scratch_shapes=slot_scratch(8, 24),
        compiler_params=pltpu.CompilerParams(vmem_limit_bytes=VMEM),
        cost_estimate=cost(SLOTS_HERE),
        name="inner_slots",
    )(centers, live, probe, *tables, field, up, down, measured)


def outer_slots(centers, live, probe, tables, field, up, down, measured, halos, partial):
    return pl.pallas_call(
        outer_kernel,
        out_shape=TILE_OUT
        + (shaped(2, TILE, HALF),) * 2
        + (shaped(2, HALF, 2 * HALF),) * 2,
        in_specs=[SMEM_SPEC] * 2 + [VMEM_SPEC] * 4 + [HBM_SPEC] * 4 + [HBM_SPEC] * 9 + [VMEM_SPEC, SMEM_SPEC],
        out_specs=(HBM_SPEC, HBM_SPEC, HBM_SPEC, VMEM_SPEC, SMEM_SPEC) + (HBM_SPEC,) * 4,
        scratch_shapes=slot_scratch(6, 34),
        input_output_aliases={16: 0, 17: 1, 18: 2},
        compiler_params=pltpu.CompilerParams(vmem_limit_bytes=VMEM),
        cost_estimate=cost(SLOTS_HERE // 2),
        name="outer_slots",
    )(centers, live, probe, *tables, field, up, down, measured, *halos, *partial)


MESH = pl.DeviceIdType.MESH
SHARE = 8
PIECES = CORE // HALF
ROW_PIECES = 4
ROW_STEP = HALF // ROW_PIECES


def return_kernel(
    scale, gleft, gright, gabove, gbelow, gup, gdown, part,
    got_left, got_right, got_up, got_down, out,
    first, second, third, kept1, kept2, kept3, full, edges, from_up, from_down, relay,
    sum_send, sum_recv, strip_send, strip_recv, row_send, row_recv, relay_send, relay_recv, corner_send, corner_recv, local,
):
    gx, gy = lax.axis_index("gx"), lax.axis_index("gy")
    core = lax.rem(gx, 2)
    spot = lax.rem(lax.div(gx, 2), 4)
    upper = lax.div(gx, 8)
    group = upper * 8 + gy
    odd = lax.rem(gy, 2)
    has_up, has_down, has_left, has_right = gx > 0, gx < 15, gy > 0, gy < 7
    crosses = gx == 8
    relays = ((gx == 7) & (odd == 1)) | ((gx == 8) & (odd == 0))
    cross_target = (jnp.where(odd == 0, 7, 8), jnp.where(odd == 0, gy + 1, gy - 1))
    relay_target = (7, jnp.where(gx == 7, gy - 1, gy + 1))
    up, down, left, right = (gx - 1, gy), (gx + 1, gy), (gx, gy - 1), (gx, gy + 1)
    far_pair = (15 - gx, jnp.where(gx == 7, gy - 1, gy + 1))

    def at_spot(k):
        return (gx + 2 * (k - spot), gy)

    def at_group(k):
        return (gx + 8 * (lax.div(k, 8) - upper), lax.rem(k, 8))

    other = (gx + 1 - 2 * core, gy)
    spots = [lax.rem(spot + d, 4) for d in range(1, 4)]
    groups = [lax.rem(group + d, 16) for d in range(1, 16)]
    barrier = pltpu.get_barrier_semaphore()

    def greet(device):
        pl.semaphore_signal(barrier, inc=1, device_id=device, device_id_type=MESH)

    sides = ((has_up, up), (has_down, down), (has_left, left), (has_right, right), (relays, far_pair))
    for there, device in sides:
        pl.when(there)(functools.partial(greet, device))
    always = [other] + [at_spot(k) for k in spots] + [at_group(k) for k in groups]
    for device in always:
        greet(device)
    expected = len(always)
    for there, _ in sides:
        expected = expected + there.astype(jnp.int32)
    pl.semaphore_wait(barrier, expected)

    def remote(source, target, send_sem, recv_sem, device):
        return pltpu.make_async_remote_copy(
            src_ref=source, dst_ref=target, send_sem=send_sem, recv_sem=recv_sem, device_id=device, device_id_type=MESH
        )

    corner_up = remote(gabove, from_down, corner_send.at[0], corner_recv.at[0], up)
    corner_down = remote(gbelow, from_up, corner_send.at[1], corner_recv.at[1], down)
    pl.when(has_up)(corner_up.start)
    pl.when(has_down)(corner_down.start)
    strips = (gleft, gright)
    loads = [
        pltpu.make_async_copy(strips[side].at[:, pl.ds(at, HALF)], edges.at[side, :, pl.ds(to, HALF)], local.at[2 * side + i])
        for side in range(2)
        for i, (at, to) in enumerate(((0, 0), (TILE - HALF, HALF)))
    ]
    for copy in loads:
        copy.start()

    def strip_copy(side, piece):
        if piece < PIECES:
            source = strips[side].at[:, pl.ds(HALF * (piece + 1), HALF)]
            place = HALF * (piece + 1)
        else:
            end = piece - PIECES
            source = edges.at[side, :, pl.ds(HALF * end, HALF)]
            place = (TILE - HALF) * end
        target = (got_right, got_left)[side].at[:, pl.ds(place, HALF)]
        return remote(source, target, strip_send.at[side, piece], strip_recv.at[side, piece], (left, right)[side])

    def strip_start(piece):
        pl.when(has_left)(lambda: strip_copy(0, piece).start())
        pl.when(has_right)(lambda: strip_copy(1, piece).start())

    def strip_sent(piece):
        pl.when(has_left)(lambda: strip_copy(0, piece).wait_send())
        pl.when(has_right)(lambda: strip_copy(1, piece).wait_send())

    def strip_got(piece):
        pl.when(has_right)(lambda: strip_copy(0, piece).wait_recv())
        pl.when(has_left)(lambda: strip_copy(1, piece).wait_recv())

    def row_rows(piece):
        return pl.ds(ROW_STEP * piece, ROW_STEP)

    def row_up(piece, direct):
        source = gup.at[:, row_rows(piece)]
        if direct:
            return remote(source, got_down.at[:, row_rows(piece)], row_send.at[0, piece], row_recv.at[0, piece], up)
        return remote(source, relay.at[:, row_rows(piece)], row_send.at[0, piece], relay_recv.at[piece], cross_target)

    def row_forward(piece):
        return remote(
            relay.at[:, row_rows(piece)], got_down.at[:, row_rows(piece)], relay_send.at[piece], row_recv.at[0, piece], relay_target
        )

    def row_down(piece):
        rows = row_rows(piece)
        return remote(gdown.at[:, rows], got_up.at[:, rows], row_send.at[1, piece], row_recv.at[1, piece], down)

    straight = has_up & (gx != 8)

    def row_start(piece):
        pl.when(straight)(lambda: row_up(piece, True).start())
        pl.when(crosses)(lambda: row_up(piece, False).start())
        pl.when(has_down)(lambda: row_down(piece).start())

    def relay_on(piece):
        def go():
            row_up(piece, False).wait_recv()
            row_forward(piece).start()

        pl.when(relays)(go)

    def rows(start, size):
        return pl.ds(pl.multiple_of(start, 8), size)

    count = [0]

    def send(source, target, device):
        i = count[0]
        count[0] += 1
        copy = remote(source, target, sum_send.at[i], sum_recv.at[i], device)
        copy.start()
        return copy

    def arrive(copies):
        for copy in copies:
            copy.wait_recv()

    strip_start(0)
    stage = [send(part.at[rows((1 - core) * 512, 512)], first, other)]
    sent = list(stage)
    row_start(0)
    strip_start(1)
    arrive(stage)
    kept1[...] = part[rows(core * 512, 512), :] + first[...]
    stage = [send(kept1.at[rows(k * 128, 128)], second.at[d], at_spot(k)) for d, k in enumerate(spots)]
    sent += stage
    for copy in loads:
        copy.wait()

    @pl.when(has_down)
    def _():
        corner_up.wait_recv()
        for side in range(2):
            edges[side, :, HALF:] += from_down[:, :, HALF * side : HALF * (side + 1)]

    @pl.when(has_up)
    def _():
        corner_down.wait_recv()
        for side in range(2):
            edges[side, :, :HALF] += from_up[:, :, HALF * side : HALF * (side + 1)]

    row_start(1)
    strip_start(2)
    strip_sent(0)
    arrive(stage)
    kept2[...] = kept1[rows(spot * 128, 128), :] + (second[0] + second[1] + second[2])
    stage = [send(kept2.at[rows(k * SHARE, SHARE)], third.at[d], at_group(k)) for d, k in enumerate(groups)]
    sent += stage
    relay_on(0)
    row_start(2)
    strip_start(3)
    strip_sent(1)
    arrive(stage)
    total = kept2[rows(group * SHARE, SHARE), :]
    for d in range(15):
        total = total + third[d]
    kept3[...] = total * scale
    mine = rows(core * 512 + spot * 128 + group * SHARE, SHARE)
    full[mine, :] = kept3[...]
    stage = [send(kept3, full.at[mine], at_group(k)) for k in groups]
    sent += stage
    relay_on(1)
    row_start(3)
    strip_start(4)
    strip_sent(2)
    arrive(stage)
    quarter = full.at[rows(core * 512 + spot * 128, 128)]
    stage = [send(quarter, quarter, at_spot(k)) for k in spots]
    sent += stage
    relay_on(2)
    strip_start(5)
    strip_sent(3)
    arrive(stage)
    whole = full.at[rows(core * 512, 512)]
    stage = [send(whole, whole, other)]
    sent += stage
    relay_on(3)
    strip_start(6)
    strip_start(7)
    arrive(stage)
    for part_at in range(2):
        for side in range(2):
            out[part_at, :, HALF * side : HALF * (side + 1)] = full[pl.ds((part_at * 2 + side) * M, M), :]
    for piece in range(4, PIECES + 2):
        strip_sent(piece)
    for piece in range(PIECES + 2):
        strip_got(piece)
    for piece in range(ROW_PIECES):
        pl.when(has_down)(lambda: row_down(piece).wait_send())
        pl.when(has_up)(lambda: row_up(piece, True).wait_send())
        pl.when(relays)(lambda: row_forward(piece).wait_send())
        pl.when(has_down)(lambda: row_up(piece, True).wait_recv())
        pl.when(has_up)(lambda: row_down(piece).wait_recv())
    pl.when(has_up)(corner_up.wait_send)
    pl.when(has_down)(corner_down.wait_send)
    for copy in sent:
        copy.wait_send()


def send_back(gleft, gright, gabove, gbelow, gup, gdown, part, scale):
    copies = 2 * (1 + 3 + 15)
    return pl.pallas_call(
        functools.partial(return_kernel, scale),
        out_shape=(shaped(2, TILE, HALF),) * 2 + (shaped(2, HALF, TILE),) * 2 + (shaped(2, M, M),),
        in_specs=[HBM_SPEC] * 6 + [VMEM_SPEC],
        out_specs=(HBM_SPEC,) * 4 + (VMEM_SPEC,),
        scratch_shapes=[
            pltpu.VMEM((512, HALF), jnp.float32),
            pltpu.VMEM((3, 128, HALF), jnp.float32),
            pltpu.VMEM((15, SHARE, HALF), jnp.float32),
            pltpu.VMEM((512, HALF), jnp.float32),
            pltpu.VMEM((128, HALF), jnp.float32),
            pltpu.VMEM((SHARE, HALF), jnp.float32),
            pltpu.VMEM((1024, HALF), jnp.float32),
            pltpu.VMEM((2, 2, 2 * HALF, HALF), jnp.float32),
            pltpu.VMEM((2, HALF, 2 * HALF), jnp.float32),
            pltpu.VMEM((2, HALF, 2 * HALF), jnp.float32),
            pltpu.VMEM((2, HALF, TILE), jnp.float32),
            pltpu.SemaphoreType.DMA((copies,)),
            pltpu.SemaphoreType.DMA((copies,)),
            pltpu.SemaphoreType.DMA((2, PIECES + 2)),
            pltpu.SemaphoreType.DMA((2, PIECES + 2)),
            pltpu.SemaphoreType.DMA((2, ROW_PIECES)),
            pltpu.SemaphoreType.DMA((2, ROW_PIECES)),
            pltpu.SemaphoreType.DMA((ROW_PIECES,)),
            pltpu.SemaphoreType.DMA((ROW_PIECES,)),
            pltpu.SemaphoreType.DMA((2,)),
            pltpu.SemaphoreType.DMA((2,)),
            pltpu.SemaphoreType.DMA((4,)),
        ],
        compiler_params=pltpu.CompilerParams(collective_id=0, has_side_effects=True, vmem_limit_bytes=VMEM),
        cost_estimate=pl.CostEstimate(flops=M * M * 8, bytes_accessed=100 << 20, transcendentals=0),
        name="send_back",
    )(gleft, gright, gabove, gbelow, gup, gdown, part.reshape(1024, HALF))


def fold_kernel(got_left, got_right, got_up, got_down, tile, out, band, side_band, row_in, strip_in, sems):
    gx, gy = lax.axis_index("gx"), lax.axis_index("gy")
    end = TILE - HALF
    frame = [
        (tile.at[:, pl.ds(0, HALF)], band.at[0]),
        (tile.at[:, pl.ds(end, HALF)], band.at[1]),
        (tile.at[:, pl.ds(HALF, CORE), pl.ds(0, HALF)], side_band.at[0]),
        (tile.at[:, pl.ds(HALF, CORE), pl.ds(end, HALF)], side_band.at[1]),
    ]
    arrived = [(got_up, row_in.at[0]), (got_down, row_in.at[1]), (got_left, strip_in.at[0]), (got_right, strip_in.at[1])]
    loads = start_all(frame + arrived, sems)
    wait_all(loads)
    for i, there in enumerate((gx > 0, gx < 15)):
        @pl.when(there)
        def _():
            band[i] += row_in[i]

    for i, there in enumerate((gy > 0, gy < 7)):
        lanes = slice(end * i, end * i + HALF)

        @pl.when(there)
        def _():
            band[0, :, :, lanes] += strip_in[i, :, :HALF]
            side_band[i] += strip_in[i, :, HALF:end]
            band[1, :, :, lanes] += strip_in[i, :, end:]

    back = [
        (band.at[0], out.at[:, pl.ds(0, HALF)]),
        (band.at[1], out.at[:, pl.ds(end, HALF)]),
        (side_band.at[0], out.at[:, pl.ds(HALF, CORE), pl.ds(0, HALF)]),
        (side_band.at[1], out.at[:, pl.ds(HALF, CORE), pl.ds(end, HALF)]),
    ]
    wait_all(start_all(back, sems))


def fold(tile, got_left, got_right, got_up, got_down):
    return pl.pallas_call(
        fold_kernel,
        out_shape=shaped(2, TILE, TILE),
        in_specs=[HBM_SPEC] * 5,
        out_specs=HBM_SPEC,
        scratch_shapes=[
            pltpu.VMEM((2, 2, HALF, TILE), jnp.float32),
            pltpu.VMEM((2, 2, CORE, HALF), jnp.float32),
            pltpu.VMEM((2, 2, HALF, TILE), jnp.float32),
            pltpu.VMEM((2, 2, TILE, HALF), jnp.float32),
            pltpu.SemaphoreType.DMA((8,)),
        ],
        input_output_aliases={4: 0},
        compiler_params=pltpu.CompilerParams(vmem_limit_bytes=VMEM),
        name="fold",
    )(got_left, got_right, got_up, got_down, tile)


def shift_by_one(x, axis, forward):
    count = lax.axis_size(axis)
    steps = [(i, i + 1) if forward else (i + 1, i) for i in range(count - 1)]
    return lax.ppermute(x, axis, steps)


def to_right(x):
    return shift_by_one(x, "gy", True)


def to_left(x):
    return shift_by_one(x, "gy", False)


def to_down(x):
    return shift_by_one(x, "gx", True)


def to_up(x):
    return shift_by_one(x, "gx", False)


def joint(x, pairs):
    return lax.ppermute(x, ("gx", "gy"), [(8 * a + b, 8 * c + d) for (a, b), (c, d) in pairs])


def to_up_relayed(x):
    straight = lax.ppermute(x, "gx", [(i + 1, i) for i in range(15) if i != 7])
    once = joint(
        x, [((8, 2 * y), (7, 2 * y + 1)) for y in range(4)] + [((8, 2 * y + 1), (8, 2 * y)) for y in range(4)]
    )
    twice = joint(
        once, [((7, 2 * y + 1), (7, 2 * y)) for y in range(4)] + [((8, 2 * y), (7, 2 * y + 1)) for y in range(4)]
    )
    return straight + twice


def ends(strip):
    return jnp.concatenate([strip[:, :HALF], strip[:, TILE - HALF :]], axis=1)


def on_device(field, probe, centers, live, measured):
    tables = tuple(jnp.asarray(t) for t in host_tables())
    first, last = field[:, :, :HALF], field[:, :, TILE - HALF :]
    left_edge, right_edge = to_right(ends(last)), to_left(ends(first))
    left_core, right_core = to_right(last[:, HALF : TILE - HALF]), to_left(first[:, HALF : TILE - HALF])
    up, down = to_down(field[:, TILE - HALF :]), to_up_relayed(field[:, :HALF])
    above = to_down(jnp.concatenate([left_edge[:, HALF:], right_edge[:, HALF:]], axis=2))
    below = to_up(jnp.concatenate([left_edge[:, :HALF], right_edge[:, :HALF]], axis=2))
    halos = (left_edge, left_core, right_edge, right_core, above, below)
    partial = inner_slots(centers, live, probe, tables, field, up, down, measured)
    grad, gup, gdown, acc, losses, gleft, gright, gabove, gbelow = outer_slots(
        centers, live, probe, tables, field, up, down, measured, halos, partial
    )
    slots_all = SLOTS_HERE * lax.axis_size("gx") * lax.axis_size("gy")
    *got, probe_grad = send_back(gleft, gright, gabove, gbelow, gup, gdown, acc, 1.0 / math.sqrt(slots_all))
    return fold(grad, *got), probe_grad, losses


def solution(mesh):
    placed = (
        P(None, "gx", "gy"),
        P(),
        P(("gx", "gy"), None),
        P(("gx", "gy")),
        P(("gx", "gy"), None, None),
    )
    return jax.shard_map(
        on_device,
        mesh=mesh,
        in_specs=placed,
        out_specs=(P(None, "gx", "gy"), P(), P(("gx", "gy"))),
        check_vma=False,
    )
```

```python
import functools
import math

import jax
import jax.numpy as jnp
import ml_dtypes
import numpy as np
from jax import lax
from jax.experimental import pallas as pl
from jax.experimental.pallas import tpu as pltpu
from jax.sharding import PartitionSpec as P

M = 256
HALF = 128
TILE = 1024
SLOTS_HERE = 16
ROWS = TILE + 2 * HALF
VMEM = 60 * 1024 * 1024


def split_host(table):
    high = table.astype(ml_dtypes.bfloat16)
    low = (table - high.astype(np.float64)).astype(ml_dtypes.bfloat16)
    return high, low


def host_tables():
    n = np.arange(HALF)
    lefts, rights = [], []
    for odd in (0, 1):
        k = 2 * np.arange(HALF) + odd
        angle = 2.0 * np.pi * (np.outer(k, n) % M) / M
        c, s = np.cos(angle) / 16.0, np.sin(angle) / 16.0
        both = np.block([[c, s], [-s, c]])
        for table in (both, both.T):
            high, low = split_host(table)
            lefts.append(np.concatenate([high, low, high], axis=1))
            rights.append(np.concatenate([high, high, low], axis=0))
    pick = np.zeros((M, M))
    pick[2 * n, n] = 1.0
    pick[2 * n + 1, HALF + n] = 1.0
    pick = pick.astype(ml_dtypes.bfloat16)
    return np.stack(lefts), np.stack(rights), np.concatenate([pick, pick], axis=0)


def halves(x):
    high = x.astype(jnp.bfloat16)
    low = (x - high.astype(jnp.float32)).astype(jnp.bfloat16)
    return high, low


def left_product(table, x):
    high, low = halves(x)
    return jnp.dot(table, jnp.concatenate([high, high, low], axis=0), preferred_element_type=jnp.float32)


def right_product(x, table):
    high, low = halves(x)
    return jnp.dot(jnp.concatenate([high, low, high], axis=1), table, preferred_element_type=jnp.float32)


def visit(obj, grad, probe, seen, slot, lefts, rights, pick, acc, row, block, block_end, shift):
    lane = lax.broadcasted_iota(jnp.int32, (M, HALF), 1)
    wraps = lane < shift
    rows = pl.ds(row, M)

    def window(part):
        first = jnp.where(wraps, obj[part, block_end, rows, :], obj[part, block, rows, :])
        return jnp.concatenate([first, obj[part, block + 1, rows, :]], axis=1)

    obj_re, obj_im = window(0), window(1)
    probe_re = pltpu.roll(probe[0], shift, 1)
    probe_im = pltpu.roll(probe[1], shift, 1)
    wave_re = probe_re * obj_re - probe_im * obj_im
    wave_im = probe_re * obj_im + probe_im * obj_re
    top, low = slice(0, HALF), slice(HALF, M)
    even = left_product(lefts[0], jnp.concatenate([wave_re[top] + wave_re[low], wave_im[top] + wave_im[low]], axis=0))
    odd = left_product(lefts[2], jnp.concatenate([wave_re[top] - wave_re[low], wave_im[top] - wave_im[low]], axis=0))
    half_re = jnp.concatenate([even[top], odd[top]], axis=0)
    half_im = jnp.concatenate([even[low], odd[low]], axis=0)
    far_e = right_product(
        jnp.concatenate([half_re[:, top] + half_re[:, low], half_im[:, top] + half_im[:, low]], axis=1), rights[1]
    )
    far_o = right_product(
        jnp.concatenate([half_re[:, top] - half_re[:, low], half_im[:, top] - half_im[:, low]], axis=1), rights[3]
    )
    meas = jnp.concatenate(
        [
            jnp.concatenate([seen[slot, side, pl.ds(odd, HALF, stride=2), :] for side in range(2)], axis=1)
            for odd in range(2)
        ],
        axis=0,
    )
    meas = jnp.dot(jnp.concatenate(halves(meas), axis=1), pick[...], preferred_element_type=jnp.float32)

    def residual(far, seen):
        squares = far * far
        total = squares[:, top] + squares[:, low] + 1.0
        inverse = lax.rsqrt(total)
        differ = total * inverse - seen
        factor = differ * inverse
        return far * jnp.concatenate([factor, factor], axis=1), differ * differ

    back_e, loss_e = residual(far_e, meas[:, top])
    back_o, loss_o = residual(far_o, meas[:, low])
    loss = jnp.sum(loss_e + loss_o) * (0.5 / (M * M))
    up = right_product(back_e, rights[0])
    vp = right_product(back_o, rights[2])
    plus, minus = up + vp, up - vp
    half_re = jnp.concatenate([plus[:, top], minus[:, top]], axis=1)
    half_im = jnp.concatenate([plus[:, low], minus[:, low]], axis=1)
    up = left_product(lefts[1], jnp.concatenate([half_re[top], half_im[top]], axis=0))
    vp = left_product(lefts[3], jnp.concatenate([half_re[low], half_im[low]], axis=0))
    plus, minus = up + vp, up - vp
    back_re = jnp.concatenate([plus[top], minus[top]], axis=0)
    back_im = jnp.concatenate([plus[low], minus[low]], axis=0)

    grads = (probe_re * back_re + probe_im * back_im, probe_re * back_im - probe_im * back_re)
    for part, g in enumerate(grads):
        first = g[:, top]
        grad[part, block, rows, :] += jnp.where(wraps, 0.0, first)
        grad[part, block + 1, rows, :] += g[:, low]
        grad[part, block_end, rows, :] += jnp.where(wraps, first, 0.0)
    unshift = lax.rem(M - shift, M)
    terms = (obj_re * back_re + obj_im * back_im, obj_re * back_im - obj_im * back_re)
    for part, term in enumerate(terms):
        turned = pltpu.roll(term, unshift, 1)
        acc[part, 0] += turned[:, top]
        acc[part, 1] += turned[:, low]
    return loss


INNER_COST = SLOTS_HERE
CORE = TILE - 2 * HALF


def start_all(pairs, sems):
    copies = [pltpu.make_async_copy(source, target, sems.at[i]) for i, (source, target) in enumerate(pairs)]
    for copy in copies:
        copy.start()
    return copies


def wait_all(copies):
    for copy in copies:
        copy.wait()


def block_of(ref, index):
    return ref.at[:, :, pl.ds(HALF * index, HALF)]


def inner_pairs(tile, buffer, slots, first_row):
    return [(block_of(tile, block), buffer.at[:, place, pl.ds(first_row, TILE)]) for place, block in slots]


def band_pairs(up, down, buffer, slots):
    pairs = []
    for place, block in slots:
        pairs.append((block_of(up, block), buffer.at[:, place, pl.ds(0, HALF)]))
        pairs.append((block_of(down, block), buffer.at[:, place, pl.ds(HALF + TILE, HALF)]))
    return pairs


def strip_pairs(strip, above, below, side, buffer, place):
    return [
        (strip, buffer.at[:, place, pl.ds(HALF, TILE)]),
        (block_of(above, side), buffer.at[:, place, pl.ds(0, HALF)]),
        (block_of(below, side), buffer.at[:, place, pl.ds(HALF + TILE, HALF)]),
    ]


def flipped(pairs):
    return [(target, source) for source, target in pairs]


def slot_copies(measured, seen, slot_sems, s):
    return [
        pltpu.make_async_copy(measured.at[s, :, pl.ds(HALF * side, HALF)], seen.at[s, side], slot_sems.at[s, side])
        for side in range(2)
    ]


def fetch_slots(live, centers, wanted, measured, seen, slot_sems):
    def fetch(s, carry):
        @pl.when(wanted(live[s], centers[s, 0], centers[s, 1]))
        def _():
            for copy in slot_copies(measured, seen, slot_sems, s):
                copy.start()

        return carry

    lax.fori_loop(0, SLOTS_HERE, fetch, 0)


def run_slots(live, centers, wanted, offset, blocks, measured, seen, slot_sems, losses, body):
    def step(s, carry):
        row, column = centers[s, 0], centers[s, 1]

        @pl.when(wanted(live[s], row, column))
        def _():
            wait_all(slot_copies(measured, seen, slot_sems, s))
            block = lax.div(column - offset, HALF)
            losses[s] = body(s, row - offset, block, jnp.minimum(block + 2, blocks - 1), lax.rem(column - offset, HALF))

        return carry

    lax.fori_loop(0, SLOTS_HERE, step, 0)


def within(row, column):
    return (row >= HALF) & (row <= TILE - HALF) & (column >= HALF) & (column <= TILE - HALF)


def is_inner(alive, row, column):
    return (alive > 0) & within(row, column)


def is_outer(alive, row, column):
    return (alive > 0) & jnp.logical_not(within(row, column))


def inner_kernel(
    centers, live, probe, lefts, rights, pick, field, measured, grad_out, acc, losses, obj, grad, seen, sems, slot_sems
):
    slots = [(j, j) for j in range(8)]
    loads = start_all(inner_pairs(field, obj, slots, 0), sems)
    fetch_slots(live, centers, is_inner, measured, seen, slot_sems)
    grad[...] = jnp.zeros_like(grad)
    acc[...] = jnp.zeros_like(acc)
    for s in range(SLOTS_HERE):
        losses[s] = 0.0
    wait_all(loads)

    def body(s, row, block, block_end, shift):
        return visit(obj, grad, probe, seen, s, lefts, rights, pick, acc, row, block, block_end, shift)

    run_slots(live, centers, is_inner, HALF, 8, measured, seen, slot_sems, losses, body)
    wait_all(start_all(flipped(inner_pairs(grad_out, grad, slots, 0)), sems))


def outer_kernel(
    centers, live, probe, lefts, rights, pick, field, up, down, measured,
    left, right, above, below, grad_in, acc_in, losses_in,
    grad_out, acc, losses, up_out, down_out, gleft, gright, gabove, gbelow,
    obj, grad, seen, sems, slot_sems,
):
    slots = [(j + 1, j) for j in range(8)]
    loads = start_all(
        inner_pairs(field, obj, slots, HALF)
        + band_pairs(up, down, obj, slots)
        + strip_pairs(left, above, below, 0, obj, 0)
        + strip_pairs(right, above, below, 1, obj, 9)
        + inner_pairs(grad_in, grad, slots, HALF),
        sems,
    )
    fetch_slots(live, centers, is_outer, measured, seen, slot_sems)
    for place_at in (0, 9):
        grad[:, place_at] = jnp.zeros((2, ROWS, HALF), jnp.float32)
    for row_at in (0, HALF + TILE):
        grad[:, 1:9, row_at : row_at + HALF] = jnp.zeros((2, 8, HALF, HALF), jnp.float32)
    acc[...] = acc_in[...]
    for s in range(SLOTS_HERE):
        losses[s] = losses_in[s]
    wait_all(loads)

    def body(s, row, block, block_end, shift):
        return visit(obj, grad, probe, seen, s, lefts, rights, pick, acc, row, block, block_end, shift)

    run_slots(live, centers, is_outer, 0, 10, measured, seen, slot_sems, losses, body)
    wait_all(
        start_all(
            flipped(
                inner_pairs(grad_out, grad, slots, HALF)
                + band_pairs(up_out, down_out, grad, slots)
                + strip_pairs(gleft, gabove, gbelow, 0, grad, 0)
                + strip_pairs(gright, gabove, gbelow, 1, grad, 9)
            ),
            sems,
        )
    )


VMEM_SPEC = pl.BlockSpec(memory_space=pltpu.VMEM)
SMEM_SPEC = pl.BlockSpec(memory_space=pltpu.SMEM)
HBM_SPEC = pl.BlockSpec(memory_space=pl.ANY)


def shaped(*shape):
    return jax.ShapeDtypeStruct(shape, jnp.float32)


def slot_scratch(blocks, copies):
    return [
        pltpu.VMEM((2, blocks, HALF * blocks, HALF), jnp.float32),
        pltpu.VMEM((2, blocks, HALF * blocks, HALF), jnp.float32),
        pltpu.VMEM((SLOTS_HERE, 2, M, HALF), jnp.float32),
        pltpu.SemaphoreType.DMA((copies,)),
        pltpu.SemaphoreType.DMA((SLOTS_HERE, 2)),
    ]


def cost(slots):
    return pl.CostEstimate(flops=slots * 26 * 2 * M**3, bytes_accessed=30 << 20, transcendentals=slots * M * M)


TILE_OUT = (shaped(2, TILE, TILE), shaped(2, 2, M, HALF), shaped(SLOTS_HERE))
TILE_SPECS = (HBM_SPEC, VMEM_SPEC, SMEM_SPEC)


def inner_slots(centers, live, probe, tables, field, measured):
    return pl.pallas_call(
        inner_kernel,
        out_shape=TILE_OUT,
        in_specs=[SMEM_SPEC] * 2 + [VMEM_SPEC] * 4 + [HBM_SPEC] * 2,
        out_specs=TILE_SPECS,
        scratch_shapes=slot_scratch(8, 8),
        compiler_params=pltpu.CompilerParams(vmem_limit_bytes=VMEM),
        cost_estimate=cost(INNER_COST),
        name="inner_slots",
    )(centers, live, probe, *tables, field, measured)


def outer_slots(centers, live, probe, tables, field, up, down, measured, halos, partial):
    return pl.pallas_call(
        outer_kernel,
        out_shape=TILE_OUT + (shaped(2, HALF, TILE),) * 2 + (shaped(2, TILE, HALF),) * 2 + (shaped(2, HALF, 2 * HALF),) * 2,
        in_specs=[SMEM_SPEC] * 2 + [VMEM_SPEC] * 4 + [HBM_SPEC] * 9 + [VMEM_SPEC, SMEM_SPEC],
        out_specs=TILE_SPECS + (HBM_SPEC,) * 6,
        scratch_shapes=slot_scratch(10, 38),
        input_output_aliases={14: 0},
        compiler_params=pltpu.CompilerParams(vmem_limit_bytes=VMEM),
        cost_estimate=cost(SLOTS_HERE // 2),
        name="outer_slots",
    )(centers, live, probe, *tables, field, up, down, measured, *halos, *partial)


MESH = pl.DeviceIdType.MESH
SHARE = 8
PIECES = CORE // HALF
ROW_PIECES = 4
ROW_STEP = HALF // ROW_PIECES


def return_kernel(
    scale, gleft, gright, gabove, gbelow, gup, gdown, part,
    got_left, got_right, got_up, got_down, out,
    first, second, third, kept1, kept2, kept3, full, edges, from_up, from_down, relay,
    sum_send, sum_recv, strip_send, strip_recv, row_send, row_recv, relay_send, relay_recv, corner_send, corner_recv, local,
):
    gx, gy = lax.axis_index("gx"), lax.axis_index("gy")
    core = lax.rem(gx, 2)
    spot = lax.rem(lax.div(gx, 2), 4)
    upper = lax.div(gx, 8)
    group = upper * 8 + gy
    odd = lax.rem(gy, 2)
    has_up, has_down, has_left, has_right = gx > 0, gx < 15, gy > 0, gy < 7
    crosses = gx == 8
    relays = ((gx == 7) & (odd == 1)) | ((gx == 8) & (odd == 0))
    cross_target = (jnp.where(odd == 0, 7, 8), jnp.where(odd == 0, gy + 1, gy - 1))
    relay_target = (7, jnp.where(gx == 7, gy - 1, gy + 1))
    up, down, left, right = (gx - 1, gy), (gx + 1, gy), (gx, gy - 1), (gx, gy + 1)
    far_pair = (15 - gx, jnp.where(gx == 7, gy - 1, gy + 1))

    def at_spot(k):
        return (gx + 2 * (k - spot), gy)

    def at_group(k):
        return (gx + 8 * (lax.div(k, 8) - upper), lax.rem(k, 8))

    other = (gx + 1 - 2 * core, gy)
    spots = [lax.rem(spot + d, 4) for d in range(1, 4)]
    groups = [lax.rem(group + d, 16) for d in range(1, 16)]
    barrier = pltpu.get_barrier_semaphore()

    def greet(device):
        pl.semaphore_signal(barrier, inc=1, device_id=device, device_id_type=MESH)

    sides = ((has_up, up), (has_down, down), (has_left, left), (has_right, right), (relays, far_pair))
    for there, device in sides:
        pl.when(there)(functools.partial(greet, device))
    always = [other] + [at_spot(k) for k in spots] + [at_group(k) for k in groups]
    for device in always:
        greet(device)
    expected = len(always)
    for there, _ in sides:
        expected = expected + there.astype(jnp.int32)
    pl.semaphore_wait(barrier, expected)

    def remote(source, target, send_sem, recv_sem, device):
        return pltpu.make_async_remote_copy(
            src_ref=source, dst_ref=target, send_sem=send_sem, recv_sem=recv_sem, device_id=device, device_id_type=MESH
        )

    corner_up = remote(gabove, from_down, corner_send.at[0], corner_recv.at[0], up)
    corner_down = remote(gbelow, from_up, corner_send.at[1], corner_recv.at[1], down)
    pl.when(has_up)(corner_up.start)
    pl.when(has_down)(corner_down.start)
    strips = (gleft, gright)
    loads = [
        pltpu.make_async_copy(strips[side].at[:, pl.ds(at, HALF)], edges.at[side, :, pl.ds(to, HALF)], local.at[2 * side + i])
        for side in range(2)
        for i, (at, to) in enumerate(((0, 0), (TILE - HALF, HALF)))
    ]
    for copy in loads:
        copy.start()

    def strip_copy(side, piece):
        if piece < PIECES:
            source = strips[side].at[:, pl.ds(HALF * (piece + 1), HALF)]
            place = HALF * (piece + 1)
        else:
            end = piece - PIECES
            source = edges.at[side, :, pl.ds(HALF * end, HALF)]
            place = (TILE - HALF) * end
        target = (got_right, got_left)[side].at[:, pl.ds(place, HALF)]
        return remote(source, target, strip_send.at[side, piece], strip_recv.at[side, piece], (left, right)[side])

    def strip_start(piece):
        pl.when(has_left)(lambda: strip_copy(0, piece).start())
        pl.when(has_right)(lambda: strip_copy(1, piece).start())

    def strip_sent(piece):
        pl.when(has_left)(lambda: strip_copy(0, piece).wait_send())
        pl.when(has_right)(lambda: strip_copy(1, piece).wait_send())

    def strip_got(piece):
        pl.when(has_right)(lambda: strip_copy(0, piece).wait_recv())
        pl.when(has_left)(lambda: strip_copy(1, piece).wait_recv())

    def row_rows(piece):
        return pl.ds(ROW_STEP * piece, ROW_STEP)

    def row_up(piece, direct):
        source = gup.at[:, row_rows(piece)]
        if direct:
            return remote(source, got_down.at[:, row_rows(piece)], row_send.at[0, piece], row_recv.at[0, piece], up)
        return remote(source, relay.at[:, row_rows(piece)], row_send.at[0, piece], relay_recv.at[piece], cross_target)

    def row_forward(piece):
        return remote(
            relay.at[:, row_rows(piece)], got_down.at[:, row_rows(piece)], relay_send.at[piece], row_recv.at[0, piece], relay_target
        )

    def row_down(piece):
        rows = row_rows(piece)
        return remote(gdown.at[:, rows], got_up.at[:, rows], row_send.at[1, piece], row_recv.at[1, piece], down)

    straight = has_up & (gx != 8)

    def row_start(piece):
        pl.when(straight)(lambda: row_up(piece, True).start())
        pl.when(crosses)(lambda: row_up(piece, False).start())
        pl.when(has_down)(lambda: row_down(piece).start())

    def relay_on(piece):
        def go():
            row_up(piece, False).wait_recv()
            row_forward(piece).start()

        pl.when(relays)(go)

    def rows(start, size):
        return pl.ds(pl.multiple_of(start, 8), size)

    count = [0]

    def send(source, target, device):
        i = count[0]
        count[0] += 1
        copy = remote(source, target, sum_send.at[i], sum_recv.at[i], device)
        copy.start()
        return copy

    def arrive(copies):
        for copy in copies:
            copy.wait_recv()

    strip_start(0)
    stage = [send(part.at[rows((1 - core) * 512, 512)], first, other)]
    sent = list(stage)
    row_start(0)
    strip_start(1)
    arrive(stage)
    kept1[...] = part[rows(core * 512, 512), :] + first[...]
    stage = [send(kept1.at[rows(k * 128, 128)], second.at[d], at_spot(k)) for d, k in enumerate(spots)]
    sent += stage
    for copy in loads:
        copy.wait()

    @pl.when(has_down)
    def _():
        corner_up.wait_recv()
        for side in range(2):
            edges[side, :, HALF:] += from_down[:, :, HALF * side : HALF * (side + 1)]

    @pl.when(has_up)
    def _():
        corner_down.wait_recv()
        for side in range(2):
            edges[side, :, :HALF] += from_up[:, :, HALF * side : HALF * (side + 1)]

    row_start(1)
    strip_start(2)
    strip_sent(0)
    arrive(stage)
    kept2[...] = kept1[rows(spot * 128, 128), :] + (second[0] + second[1] + second[2])
    stage = [send(kept2.at[rows(k * SHARE, SHARE)], third.at[d], at_group(k)) for d, k in enumerate(groups)]
    sent += stage
    relay_on(0)
    row_start(2)
    strip_start(3)
    strip_sent(1)
    arrive(stage)
    total = kept2[rows(group * SHARE, SHARE), :]
    for d in range(15):
        total = total + third[d]
    kept3[...] = total * scale
    mine = rows(core * 512 + spot * 128 + group * SHARE, SHARE)
    full[mine, :] = kept3[...]
    stage = [send(kept3, full.at[mine], at_group(k)) for k in groups]
    sent += stage
    relay_on(1)
    row_start(3)
    strip_start(4)
    strip_sent(2)
    arrive(stage)
    quarter = full.at[rows(core * 512 + spot * 128, 128)]
    stage = [send(quarter, quarter, at_spot(k)) for k in spots]
    sent += stage
    relay_on(2)
    strip_start(5)
    strip_sent(3)
    arrive(stage)
    whole = full.at[rows(core * 512, 512)]
    stage = [send(whole, whole, other)]
    sent += stage
    relay_on(3)
    strip_start(6)
    strip_start(7)
    arrive(stage)
    for part_at in range(2):
        for side in range(2):
            out[part_at, :, HALF * side : HALF * (side + 1)] = full[pl.ds((part_at * 2 + side) * M, M), :]
    for piece in range(4, PIECES + 2):
        strip_sent(piece)
    for piece in range(PIECES + 2):
        strip_got(piece)
    for piece in range(ROW_PIECES):
        pl.when(has_down)(lambda: row_down(piece).wait_send())
        pl.when(has_up)(lambda: row_up(piece, True).wait_send())
        pl.when(relays)(lambda: row_forward(piece).wait_send())
        pl.when(has_down)(lambda: row_up(piece, True).wait_recv())
        pl.when(has_up)(lambda: row_down(piece).wait_recv())
    pl.when(has_up)(corner_up.wait_send)
    pl.when(has_down)(corner_down.wait_send)
    for copy in sent:
        copy.wait_send()


def send_back(gleft, gright, gabove, gbelow, gup, gdown, part, scale):
    copies = 2 * (1 + 3 + 15)
    return pl.pallas_call(
        functools.partial(return_kernel, scale),
        out_shape=(shaped(2, TILE, HALF),) * 2 + (shaped(2, HALF, TILE),) * 2 + (shaped(2, M, M),),
        in_specs=[HBM_SPEC] * 6 + [VMEM_SPEC],
        out_specs=(HBM_SPEC,) * 4 + (VMEM_SPEC,),
        scratch_shapes=[
            pltpu.VMEM((512, HALF), jnp.float32),
            pltpu.VMEM((3, 128, HALF), jnp.float32),
            pltpu.VMEM((15, SHARE, HALF), jnp.float32),
            pltpu.VMEM((512, HALF), jnp.float32),
            pltpu.VMEM((128, HALF), jnp.float32),
            pltpu.VMEM((SHARE, HALF), jnp.float32),
            pltpu.VMEM((1024, HALF), jnp.float32),
            pltpu.VMEM((2, 2, 2 * HALF, HALF), jnp.float32),
            pltpu.VMEM((2, HALF, 2 * HALF), jnp.float32),
            pltpu.VMEM((2, HALF, 2 * HALF), jnp.float32),
            pltpu.VMEM((2, HALF, TILE), jnp.float32),
            pltpu.SemaphoreType.DMA((copies,)),
            pltpu.SemaphoreType.DMA((copies,)),
            pltpu.SemaphoreType.DMA((2, PIECES + 2)),
            pltpu.SemaphoreType.DMA((2, PIECES + 2)),
            pltpu.SemaphoreType.DMA((2, ROW_PIECES)),
            pltpu.SemaphoreType.DMA((2, ROW_PIECES)),
            pltpu.SemaphoreType.DMA((ROW_PIECES,)),
            pltpu.SemaphoreType.DMA((ROW_PIECES,)),
            pltpu.SemaphoreType.DMA((2,)),
            pltpu.SemaphoreType.DMA((2,)),
            pltpu.SemaphoreType.DMA((4,)),
        ],
        compiler_params=pltpu.CompilerParams(collective_id=0, has_side_effects=True, vmem_limit_bytes=VMEM),
        cost_estimate=pl.CostEstimate(flops=M * M * 8, bytes_accessed=100 << 20, transcendentals=0),
        name="send_back",
    )(gleft, gright, gabove, gbelow, gup, gdown, part.reshape(1024, HALF))


def fold_kernel(got_left, got_right, got_up, got_down, tile, out, band, side_band, row_in, strip_in, sems):
    gx, gy = lax.axis_index("gx"), lax.axis_index("gy")
    end = TILE - HALF
    frame = [
        (tile.at[:, pl.ds(0, HALF)], band.at[0]),
        (tile.at[:, pl.ds(end, HALF)], band.at[1]),
        (tile.at[:, pl.ds(HALF, CORE), pl.ds(0, HALF)], side_band.at[0]),
        (tile.at[:, pl.ds(HALF, CORE), pl.ds(end, HALF)], side_band.at[1]),
    ]
    arrived = [(got_up, row_in.at[0]), (got_down, row_in.at[1]), (got_left, strip_in.at[0]), (got_right, strip_in.at[1])]
    loads = start_all(frame + arrived, sems)
    wait_all(loads)
    for i, there in enumerate((gx > 0, gx < 15)):
        @pl.when(there)
        def _():
            band[i] += row_in[i]

    for i, there in enumerate((gy > 0, gy < 7)):
        lanes = slice(end * i, end * i + HALF)

        @pl.when(there)
        def _():
            band[0, :, :, lanes] += strip_in[i, :, :HALF]
            side_band[i] += strip_in[i, :, HALF:end]
            band[1, :, :, lanes] += strip_in[i, :, end:]

    back = [
        (band.at[0], out.at[:, pl.ds(0, HALF)]),
        (band.at[1], out.at[:, pl.ds(end, HALF)]),
        (side_band.at[0], out.at[:, pl.ds(HALF, CORE), pl.ds(0, HALF)]),
        (side_band.at[1], out.at[:, pl.ds(HALF, CORE), pl.ds(end, HALF)]),
    ]
    wait_all(start_all(back, sems))


def fold(tile, got_left, got_right, got_up, got_down):
    return pl.pallas_call(
        fold_kernel,
        out_shape=shaped(2, TILE, TILE),
        in_specs=[HBM_SPEC] * 5,
        out_specs=HBM_SPEC,
        scratch_shapes=[
            pltpu.VMEM((2, 2, HALF, TILE), jnp.float32),
            pltpu.VMEM((2, 2, CORE, HALF), jnp.float32),
            pltpu.VMEM((2, 2, HALF, TILE), jnp.float32),
            pltpu.VMEM((2, 2, TILE, HALF), jnp.float32),
            pltpu.SemaphoreType.DMA((8,)),
        ],
        input_output_aliases={4: 0},
        compiler_params=pltpu.CompilerParams(vmem_limit_bytes=VMEM),
        name="fold",
    )(got_left, got_right, got_up, got_down, tile)


def shift_by_one(x, axis, forward):
    count = lax.axis_size(axis)
    steps = [(i, i + 1) if forward else (i + 1, i) for i in range(count - 1)]
    return lax.ppermute(x, axis, steps)


def to_right(x):
    return shift_by_one(x, "gy", True)


def to_left(x):
    return shift_by_one(x, "gy", False)


def to_down(x):
    return shift_by_one(x, "gx", True)


def to_up(x):
    return shift_by_one(x, "gx", False)


def joint(x, pairs):
    return lax.ppermute(x, ("gx", "gy"), [(8 * a + b, 8 * c + d) for (a, b), (c, d) in pairs])


def crossing_first(x):
    return joint(
        x, [((8, 2 * y), (7, 2 * y + 1)) for y in range(4)] + [((8, 2 * y + 1), (8, 2 * y)) for y in range(4)]
    )


def crossing_second(x):
    return joint(x, [((7, 2 * y + 1), (7, 2 * y)) for y in range(4)] + [((8, 2 * y), (7, 2 * y + 1)) for y in range(4)])


def to_up_straight(x):
    return lax.ppermute(x, "gx", [(i + 1, i) for i in range(15) if i != 7])


def on_device(field, probe, centers, live, measured):
    tables = tuple(jnp.asarray(t) for t in host_tables())
    left, right = to_right(field[:, :, TILE - HALF :]), to_left(field[:, :, :HALF])
    top_rows = field[:, :HALF]
    relayed, up, straight = crossing_first(top_rows), to_down(field[:, TILE - HALF :]), to_up_straight(top_rows)
    grad, acc, losses = inner_slots(centers, live, probe, tables, field, measured)
    relayed, acc = lax.optimization_barrier((relayed, acc))
    second = crossing_second(relayed)
    left, right, up, straight, acc = lax.optimization_barrier((left, right, up, straight, acc))
    above = to_down(jnp.concatenate([left[:, TILE - HALF :], right[:, TILE - HALF :]], axis=2))
    below = to_up(jnp.concatenate([left[:, :HALF], right[:, :HALF]], axis=2))
    down = straight + second
    halos = (left, right, above, below)
    partial = (grad, acc, losses)
    grad, acc, losses, gup, gdown, gleft, gright, gabove, gbelow = outer_slots(
        centers, live, probe, tables, field, up, down, measured, halos, partial
    )
    slots_all = SLOTS_HERE * lax.axis_size("gx") * lax.axis_size("gy")
    *got, probe_grad = send_back(gleft, gright, gabove, gbelow, gup, gdown, acc, 1.0 / math.sqrt(slots_all))
    return fold(grad, *got), probe_grad, losses


def solution(mesh):
    placed = (
        P(None, "gx", "gy"),
        P(),
        P(("gx", "gy"), None),
        P(("gx", "gy")),
        P(("gx", "gy"), None, None),
    )
    return jax.shard_map(
        on_device,
        mesh=mesh,
        in_specs=placed,
        out_specs=(P(None, "gx", "gy"), P(), P(("gx", "gy"))),
        check_vma=False,
    )
```

```python
import functools
import math

import jax
import jax.numpy as jnp
import ml_dtypes
import numpy as np
from jax import lax
from jax.experimental import pallas as pl
from jax.experimental.pallas import tpu as pltpu
from jax.sharding import PartitionSpec as P

M = 256
HALF = 128
TILE = 1024
SLOTS_HERE = 16
ROWS = TILE + 2 * HALF
VMEM = 60 * 1024 * 1024


def split_host(table):
    high = table.astype(ml_dtypes.bfloat16)
    low = (table - high.astype(np.float64)).astype(ml_dtypes.bfloat16)
    return high, low


def host_tables():
    n = np.arange(HALF)
    lefts, rights = [], []
    for odd in (0, 1):
        k = 2 * np.arange(HALF) + odd
        angle = 2.0 * np.pi * (np.outer(k, n) % M) / M
        c, s = np.cos(angle) / 16.0, np.sin(angle) / 16.0
        both = np.block([[c, s], [-s, c]])
        for table in (both, both.T):
            high, low = split_host(table)
            lefts.append(np.concatenate([high, low, high], axis=1))
            rights.append(np.concatenate([high, high, low], axis=0))
    pick = np.zeros((M, M))
    pick[2 * n, n] = 1.0
    pick[2 * n + 1, HALF + n] = 1.0
    pick = pick.astype(ml_dtypes.bfloat16)
    return np.stack(lefts), np.stack(rights), np.concatenate([pick, pick], axis=0)


def halves(x):
    high = x.astype(jnp.bfloat16)
    low = (x - high.astype(jnp.float32)).astype(jnp.bfloat16)
    return high, low


def left_product(table, x):
    high, low = halves(x)
    return jnp.dot(table, jnp.concatenate([high, high, low], axis=0), preferred_element_type=jnp.float32)


def right_product(x, table):
    high, low = halves(x)
    return jnp.dot(jnp.concatenate([high, low, high], axis=1), table, preferred_element_type=jnp.float32)


def visit(obj, grad, probe, seen, slot, lefts, rights, pick, acc, row, block, block_end, shift, ready=None):
    lane = lax.broadcasted_iota(jnp.int32, (M, HALF), 1)
    wraps = lane < shift
    rows = pl.ds(row, M)

    def window(part):
        first = jnp.where(wraps, obj[part, block_end, rows, :], obj[part, block, rows, :])
        return jnp.concatenate([first, obj[part, block + 1, rows, :]], axis=1)

    obj_re, obj_im = window(0), window(1)
    probe_re = pltpu.roll(probe[0], shift, 1)
    probe_im = pltpu.roll(probe[1], shift, 1)
    wave_re = probe_re * obj_re - probe_im * obj_im
    wave_im = probe_re * obj_im + probe_im * obj_re
    top, low = slice(0, HALF), slice(HALF, M)
    even = left_product(lefts[0], jnp.concatenate([wave_re[top] + wave_re[low], wave_im[top] + wave_im[low]], axis=0))
    odd = left_product(lefts[2], jnp.concatenate([wave_re[top] - wave_re[low], wave_im[top] - wave_im[low]], axis=0))
    half_re = jnp.concatenate([even[top], odd[top]], axis=0)
    half_im = jnp.concatenate([even[low], odd[low]], axis=0)
    far_e = right_product(
        jnp.concatenate([half_re[:, top] + half_re[:, low], half_im[:, top] + half_im[:, low]], axis=1), rights[1]
    )
    far_o = right_product(
        jnp.concatenate([half_re[:, top] - half_re[:, low], half_im[:, top] - half_im[:, low]], axis=1), rights[3]
    )
    meas = jnp.concatenate(
        [
            jnp.concatenate([seen[slot, side, pl.ds(odd, HALF, stride=2), :] for side in range(2)], axis=1)
            for odd in range(2)
        ],
        axis=0,
    )
    meas = jnp.dot(jnp.concatenate(halves(meas), axis=1), pick[...], preferred_element_type=jnp.float32)

    def residual(far, seen):
        squares = far * far
        total = squares[:, top] + squares[:, low] + 1.0
        inverse = lax.rsqrt(total)
        differ = total * inverse - seen
        factor = differ * inverse
        return far * jnp.concatenate([factor, factor], axis=1), differ * differ

    back_e, loss_e = residual(far_e, meas[:, top])
    back_o, loss_o = residual(far_o, meas[:, low])
    loss = jnp.sum(loss_e + loss_o) * (0.5 / (M * M))
    up = right_product(back_e, rights[0])
    vp = right_product(back_o, rights[2])
    plus, minus = up + vp, up - vp
    half_re = jnp.concatenate([plus[:, top], minus[:, top]], axis=1)
    half_im = jnp.concatenate([plus[:, low], minus[:, low]], axis=1)
    up = left_product(lefts[1], jnp.concatenate([half_re[top], half_im[top]], axis=0))
    vp = left_product(lefts[3], jnp.concatenate([half_re[low], half_im[low]], axis=0))
    plus, minus = up + vp, up - vp
    back_re = jnp.concatenate([plus[top], minus[top]], axis=0)
    back_im = jnp.concatenate([plus[low], minus[low]], axis=0)

    grads = (probe_re * back_re + probe_im * back_im, probe_re * back_im - probe_im * back_re)
    if ready is not None:
        ready()
    for part, g in enumerate(grads):
        first = g[:, top]
        grad[part, block, rows, :] += jnp.where(wraps, 0.0, first)
        grad[part, block + 1, rows, :] += g[:, low]
        grad[part, block_end, rows, :] += jnp.where(wraps, first, 0.0)
    unshift = lax.rem(M - shift, M)
    terms = (obj_re * back_re + obj_im * back_im, obj_re * back_im - obj_im * back_re)
    for part, term in enumerate(terms):
        turned = pltpu.roll(term, unshift, 1)
        acc[part, 0] += turned[:, top]
        acc[part, 1] += turned[:, low]
    return loss


INNER_COST = SLOTS_HERE
CORE = TILE - 2 * HALF


def start_all(pairs, sems):
    copies = [pltpu.make_async_copy(source, target, sems.at[i]) for i, (source, target) in enumerate(pairs)]
    for copy in copies:
        copy.start()
    return copies


def wait_all(copies):
    for copy in copies:
        copy.wait()


def block_of(ref, index):
    return ref.at[:, :, pl.ds(HALF * index, HALF)]


def inner_pairs(tile, buffer, slots, first_row):
    return [(block_of(tile, block), buffer.at[:, place, pl.ds(first_row, TILE)]) for place, block in slots]


def border_pairs(tile, buffer, slots):
    pairs = []
    for place, block in slots:
        spans = ((0, TILE),) if block in (0, 1, 6, 7) else ((0, 2 * HALF), (TILE - 2 * HALF, 2 * HALF))
        for at, size in spans:
            pairs.append(
                (tile.at[:, pl.ds(at, size), pl.ds(HALF * block, HALF)], buffer.at[:, place, pl.ds(HALF + at, size)])
            )
    return pairs


def band_pairs(up, down, buffer, slots):
    pairs = []
    for place, block in slots:
        pairs.append((block_of(up, block), buffer.at[:, place, pl.ds(0, HALF)]))
        pairs.append((block_of(down, block), buffer.at[:, place, pl.ds(HALF + TILE, HALF)]))
    return pairs


def strip_pairs(strip, above, below, side, buffer, place):
    return [
        (strip, buffer.at[:, place, pl.ds(HALF, TILE)]),
        (block_of(above, side), buffer.at[:, place, pl.ds(0, HALF)]),
        (block_of(below, side), buffer.at[:, place, pl.ds(HALF + TILE, HALF)]),
    ]


def flipped(pairs):
    return [(target, source) for source, target in pairs]


def slot_copies(measured, seen, slot_sems, s):
    return [
        pltpu.make_async_copy(measured.at[s, :, pl.ds(HALF * side, HALF)], seen.at[s, side], slot_sems.at[s, side])
        for side in range(2)
    ]


def fetch_slots(live, centers, wanted, measured, seen, slot_sems):
    def fetch(s, carry):
        @pl.when(wanted(live[s], centers[s, 0], centers[s, 1]))
        def _():
            for copy in slot_copies(measured, seen, slot_sems, s):
                copy.start()

        return carry

    lax.fori_loop(0, SLOTS_HERE, fetch, 0)


def run_slots(live, centers, wanted, offset, blocks, measured, seen, slot_sems, losses, body):
    def step(s, carry):
        row, column = centers[s, 0], centers[s, 1]

        @pl.when(wanted(live[s], row, column))
        def _():
            wait_all(slot_copies(measured, seen, slot_sems, s))
            block = lax.div(column - offset, HALF)
            losses[s] = body(s, row - offset, block, jnp.minimum(block + 2, blocks - 1), lax.rem(column - offset, HALF))

        return carry

    lax.fori_loop(0, SLOTS_HERE, step, 0)


def within(row, column):
    return (row >= HALF) & (row <= TILE - HALF) & (column >= HALF) & (column <= TILE - HALF)


def is_inner(alive, row, column):
    return (alive > 0) & within(row, column)


def is_outer(alive, row, column):
    return (alive > 0) & jnp.logical_not(within(row, column))


def inner_kernel(
    centers, live, probe, lefts, rights, pick, field, measured, grad_out, acc, losses, obj, grad, seen, sems, slot_sems
):
    slots = [(j, j) for j in range(8)]
    loads = start_all(inner_pairs(field, obj, slots, 0), sems)
    fetch_slots(live, centers, is_inner, measured, seen, slot_sems)
    grad[...] = jnp.zeros_like(grad)
    acc[...] = jnp.zeros_like(acc)
    for s in range(SLOTS_HERE):
        losses[s] = 0.0
    wait_all(loads)

    def body(s, row, block, block_end, shift):
        return visit(obj, grad, probe, seen, s, lefts, rights, pick, acc, row, block, block_end, shift)

    run_slots(live, centers, is_inner, HALF, 8, measured, seen, slot_sems, losses, body)
    wait_all(start_all(flipped(inner_pairs(grad_out, grad, slots, 0)), sems))


def outer_kernel(
    centers, live, probe, lefts, rights, pick, field, up, down, measured,
    left, right, above, below, grad_in, acc_in, losses_in,
    grad_out, acc, losses, up_out, down_out, gleft, gright, gabove, gbelow,
    obj, grad, seen, sems, slot_sems, grad_sems, loaded,
):
    slots = [(j + 1, j) for j in range(8)]
    loads = start_all(
        border_pairs(field, obj, slots)
        + band_pairs(up, down, obj, slots)
        + strip_pairs(left, above, below, 0, obj, 0)
        + strip_pairs(right, above, below, 1, obj, 9),
        sems,
    )
    fetch_slots(live, centers, is_outer, measured, seen, slot_sems)
    grad_loads = start_all(border_pairs(grad_in, grad, slots), grad_sems)
    for place_at in (0, 9):
        grad[:, place_at] = jnp.zeros((2, ROWS, HALF), jnp.float32)
    for row_at in (0, HALF + TILE):
        grad[:, 1:9, row_at : row_at + HALF] = jnp.zeros((2, 8, HALF, HALF), jnp.float32)
    acc[...] = acc_in[...]
    for s in range(SLOTS_HERE):
        losses[s] = losses_in[s]
    wait_all(loads)
    loaded[0] = 0

    def have_grads():
        @pl.when(loaded[0] == 0)
        def _():
            wait_all(grad_loads)
            loaded[0] = 1

    def body(s, row, block, block_end, shift):
        return visit(obj, grad, probe, seen, s, lefts, rights, pick, acc, row, block, block_end, shift, have_grads)

    run_slots(live, centers, is_outer, 0, 10, measured, seen, slot_sems, losses, body)
    have_grads()
    wait_all(
        start_all(
            flipped(
                strip_pairs(gleft, gabove, gbelow, 0, grad, 0)
                + strip_pairs(gright, gabove, gbelow, 1, grad, 9)
                + band_pairs(up_out, down_out, grad, slots)
                + border_pairs(grad_out, grad, slots)
            ),
            sems,
        )
    )


VMEM_SPEC = pl.BlockSpec(memory_space=pltpu.VMEM)
SMEM_SPEC = pl.BlockSpec(memory_space=pltpu.SMEM)
HBM_SPEC = pl.BlockSpec(memory_space=pl.ANY)


def shaped(*shape):
    return jax.ShapeDtypeStruct(shape, jnp.float32)


def slot_scratch(blocks, copies):
    return [
        pltpu.VMEM((2, blocks, HALF * blocks, HALF), jnp.float32),
        pltpu.VMEM((2, blocks, HALF * blocks, HALF), jnp.float32),
        pltpu.VMEM((SLOTS_HERE, 2, M, HALF), jnp.float32),
        pltpu.SemaphoreType.DMA((copies,)),
        pltpu.SemaphoreType.DMA((SLOTS_HERE, 2)),
    ]


def cost(slots):
    return pl.CostEstimate(flops=slots * 26 * 2 * M**3, bytes_accessed=30 << 20, transcendentals=slots * M * M)


TILE_OUT = (shaped(2, TILE, TILE), shaped(2, 2, M, HALF), shaped(SLOTS_HERE))
TILE_SPECS = (HBM_SPEC, VMEM_SPEC, SMEM_SPEC)


def inner_slots(centers, live, probe, tables, field, measured):
    return pl.pallas_call(
        inner_kernel,
        out_shape=TILE_OUT,
        in_specs=[SMEM_SPEC] * 2 + [VMEM_SPEC] * 4 + [HBM_SPEC] * 2,
        out_specs=TILE_SPECS,
        scratch_shapes=slot_scratch(8, 8),
        compiler_params=pltpu.CompilerParams(vmem_limit_bytes=VMEM),
        cost_estimate=cost(INNER_COST),
        name="inner_slots",
    )(centers, live, probe, *tables, field, measured)


def outer_slots(centers, live, probe, tables, field, up, down, measured, halos, partial):
    return pl.pallas_call(
        outer_kernel,
        out_shape=TILE_OUT + (shaped(2, HALF, TILE),) * 2 + (shaped(2, TILE, HALF),) * 2 + (shaped(2, HALF, 2 * HALF),) * 2,
        in_specs=[SMEM_SPEC] * 2 + [VMEM_SPEC] * 4 + [HBM_SPEC] * 9 + [VMEM_SPEC, SMEM_SPEC],
        out_specs=TILE_SPECS + (HBM_SPEC,) * 6,
        scratch_shapes=slot_scratch(10, 34) + [pltpu.SemaphoreType.DMA((12,)), pltpu.SMEM((1,), jnp.int32)],
        input_output_aliases={14: 0},
        compiler_params=pltpu.CompilerParams(vmem_limit_bytes=VMEM),
        cost_estimate=cost(SLOTS_HERE // 2),
        name="outer_slots",
    )(centers, live, probe, *tables, field, up, down, measured, *halos, *partial)


MESH = pl.DeviceIdType.MESH
SHARE = 8
PIECES = CORE // HALF
ROW_PIECES = 4
ROW_STEP = HALF // ROW_PIECES


def return_kernel(
    scale, gleft, gright, gabove, gbelow, gup, gdown, part,
    got_left, got_right, got_up, got_down, out,
    first, second, third, kept1, kept2, kept3, full, edges, from_up, from_down, relay,
    sum_send, sum_recv, strip_send, strip_recv, row_send, row_recv, relay_send, relay_recv, corner_send, corner_recv, local,
):
    gx, gy = lax.axis_index("gx"), lax.axis_index("gy")
    core = lax.rem(gx, 2)
    spot = lax.rem(lax.div(gx, 2), 4)
    upper = lax.div(gx, 8)
    group = upper * 8 + gy
    odd = lax.rem(gy, 2)
    has_up, has_down, has_left, has_right = gx > 0, gx < 15, gy > 0, gy < 7
    crosses = gx == 8
    relays = ((gx == 7) & (odd == 1)) | ((gx == 8) & (odd == 0))
    cross_target = (jnp.where(odd == 0, 7, 8), jnp.where(odd == 0, gy + 1, gy - 1))
    relay_target = (7, jnp.where(gx == 7, gy - 1, gy + 1))
    up, down, left, right = (gx - 1, gy), (gx + 1, gy), (gx, gy - 1), (gx, gy + 1)
    far_pair = (15 - gx, jnp.where(gx == 7, gy - 1, gy + 1))

    def at_spot(k):
        return (gx + 2 * (k - spot), gy)

    def at_group(k):
        return (gx + 8 * (lax.div(k, 8) - upper), lax.rem(k, 8))

    other = (gx + 1 - 2 * core, gy)
    spots = [lax.rem(spot + d, 4) for d in range(1, 4)]
    groups = [lax.rem(group + d, 16) for d in range(1, 16)]
    barrier = pltpu.get_barrier_semaphore()

    def greet(device):
        pl.semaphore_signal(barrier, inc=1, device_id=device, device_id_type=MESH)

    sides = ((has_up, up), (has_down, down), (has_left, left), (has_right, right), (relays, far_pair))
    for there, device in sides:
        pl.when(there)(functools.partial(greet, device))
    always = [other] + [at_spot(k) for k in spots] + [at_group(k) for k in groups]
    for device in always:
        greet(device)
    expected = len(always)
    for there, _ in sides:
        expected = expected + there.astype(jnp.int32)
    pl.semaphore_wait(barrier, expected)

    def remote(source, target, send_sem, recv_sem, device):
        return pltpu.make_async_remote_copy(
            src_ref=source, dst_ref=target, send_sem=send_sem, recv_sem=recv_sem, device_id=device, device_id_type=MESH
        )

    corner_up = remote(gabove, from_down, corner_send.at[0], corner_recv.at[0], up)
    corner_down = remote(gbelow, from_up, corner_send.at[1], corner_recv.at[1], down)
    pl.when(has_up)(corner_up.start)
    pl.when(has_down)(corner_down.start)
    strips = (gleft, gright)
    loads = [
        pltpu.make_async_copy(strips[side].at[:, pl.ds(at, HALF)], edges.at[side, :, pl.ds(to, HALF)], local.at[2 * side + i])
        for side in range(2)
        for i, (at, to) in enumerate(((0, 0), (TILE - HALF, HALF)))
    ]
    for copy in loads:
        copy.start()

    def strip_copy(side, piece):
        if piece < PIECES:
            source = strips[side].at[:, pl.ds(HALF * (piece + 1), HALF)]
            place = HALF * (piece + 1)
        else:
            end = piece - PIECES
            source = edges.at[side, :, pl.ds(HALF * end, HALF)]
            place = (TILE - HALF) * end
        target = (got_right, got_left)[side].at[:, pl.ds(place, HALF)]
        return remote(source, target, strip_send.at[side, piece], strip_recv.at[side, piece], (left, right)[side])

    def strip_start(piece):
        pl.when(has_left)(lambda: strip_copy(0, piece).start())
        pl.when(has_right)(lambda: strip_copy(1, piece).start())

    def strip_sent(piece):
        pl.when(has_left)(lambda: strip_copy(0, piece).wait_send())
        pl.when(has_right)(lambda: strip_copy(1, piece).wait_send())

    def strip_got(piece):
        pl.when(has_right)(lambda: strip_copy(0, piece).wait_recv())
        pl.when(has_left)(lambda: strip_copy(1, piece).wait_recv())

    def row_rows(piece):
        return pl.ds(ROW_STEP * piece, ROW_STEP)

    def row_up(piece, direct):
        source = gup.at[:, row_rows(piece)]
        if direct:
            return remote(source, got_down.at[:, row_rows(piece)], row_send.at[0, piece], row_recv.at[0, piece], up)
        return remote(source, relay.at[:, row_rows(piece)], row_send.at[0, piece], relay_recv.at[piece], cross_target)

    def row_forward(piece):
        return remote(
            relay.at[:, row_rows(piece)], got_down.at[:, row_rows(piece)], relay_send.at[piece], row_recv.at[0, piece], relay_target
        )

    def row_down(piece):
        rows = row_rows(piece)
        return remote(gdown.at[:, rows], got_up.at[:, rows], row_send.at[1, piece], row_recv.at[1, piece], down)

    straight = has_up & (gx != 8)

    def row_start(piece):
        pl.when(straight)(lambda: row_up(piece, True).start())
        pl.when(crosses)(lambda: row_up(piece, False).start())
        pl.when(has_down)(lambda: row_down(piece).start())

    def relay_on(piece):
        def go():
            row_up(piece, False).wait_recv()
            row_forward(piece).start()

        pl.when(relays)(go)

    def rows(start, size):
        return pl.ds(pl.multiple_of(start, 8), size)

    count = [0]

    def send(source, target, device):
        i = count[0]
        count[0] += 1
        copy = remote(source, target, sum_send.at[i], sum_recv.at[i], device)
        copy.start()
        return copy

    def arrive(copies):
        for copy in copies:
            copy.wait_recv()

    strip_start(0)
    stage = [send(part.at[rows((1 - core) * 512, 512)], first, other)]
    sent = list(stage)
    row_start(0)
    strip_start(1)
    arrive(stage)
    kept1[...] = part[rows(core * 512, 512), :] + first[...]
    stage = [send(kept1.at[rows(k * 128, 128)], second.at[d], at_spot(k)) for d, k in enumerate(spots)]
    sent += stage
    for copy in loads:
        copy.wait()

    @pl.when(has_down)
    def _():
        corner_up.wait_recv()
        for side in range(2):
            edges[side, :, HALF:] += from_down[:, :, HALF * side : HALF * (side + 1)]

    @pl.when(has_up)
    def _():
        corner_down.wait_recv()
        for side in range(2):
            edges[side, :, :HALF] += from_up[:, :, HALF * side : HALF * (side + 1)]

    row_start(1)
    strip_start(2)
    strip_sent(0)
    arrive(stage)
    kept2[...] = kept1[rows(spot * 128, 128), :] + (second[0] + second[1] + second[2])
    stage = [send(kept2.at[rows(k * SHARE, SHARE)], third.at[d], at_group(k)) for d, k in enumerate(groups)]
    sent += stage
    relay_on(0)
    row_start(2)
    strip_start(3)
    strip_sent(1)
    arrive(stage)
    total = kept2[rows(group * SHARE, SHARE), :]
    for d in range(15):
        total = total + third[d]
    kept3[...] = total * scale
    mine = rows(core * 512 + spot * 128 + group * SHARE, SHARE)
    full[mine, :] = kept3[...]
    stage = [send(kept3, full.at[mine], at_group(k)) for k in groups]
    sent += stage
    relay_on(1)
    row_start(3)
    strip_start(4)
    strip_sent(2)
    arrive(stage)
    quarter = full.at[rows(core * 512 + spot * 128, 128)]
    stage = [send(quarter, quarter, at_spot(k)) for k in spots]
    sent += stage
    relay_on(2)
    strip_start(5)
    strip_sent(3)
    arrive(stage)
    whole = full.at[rows(core * 512, 512)]
    stage = [send(whole, whole, other)]
    sent += stage
    relay_on(3)
    strip_start(6)
    strip_start(7)
    arrive(stage)
    for part_at in range(2):
        for side in range(2):
            out[part_at, :, HALF * side : HALF * (side + 1)] = full[pl.ds((part_at * 2 + side) * M, M), :]
    for piece in range(4, PIECES + 2):
        strip_sent(piece)
    for piece in range(PIECES + 2):
        strip_got(piece)
    for piece in range(ROW_PIECES):
        pl.when(has_down)(lambda: row_down(piece).wait_send())
        pl.when(has_up)(lambda: row_up(piece, True).wait_send())
        pl.when(relays)(lambda: row_forward(piece).wait_send())
        pl.when(has_down)(lambda: row_up(piece, True).wait_recv())
        pl.when(has_up)(lambda: row_down(piece).wait_recv())
    pl.when(has_up)(corner_up.wait_send)
    pl.when(has_down)(corner_down.wait_send)
    for copy in sent:
        copy.wait_send()


def send_back(gleft, gright, gabove, gbelow, gup, gdown, part, scale):
    copies = 2 * (1 + 3 + 15)
    return pl.pallas_call(
        functools.partial(return_kernel, scale),
        out_shape=(shaped(2, TILE, HALF),) * 2 + (shaped(2, HALF, TILE),) * 2 + (shaped(2, M, M),),
        in_specs=[HBM_SPEC] * 6 + [VMEM_SPEC],
        out_specs=(HBM_SPEC,) * 4 + (VMEM_SPEC,),
        scratch_shapes=[
            pltpu.VMEM((512, HALF), jnp.float32),
            pltpu.VMEM((3, 128, HALF), jnp.float32),
            pltpu.VMEM((15, SHARE, HALF), jnp.float32),
            pltpu.VMEM((512, HALF), jnp.float32),
            pltpu.VMEM((128, HALF), jnp.float32),
            pltpu.VMEM((SHARE, HALF), jnp.float32),
            pltpu.VMEM((1024, HALF), jnp.float32),
            pltpu.VMEM((2, 2, 2 * HALF, HALF), jnp.float32),
            pltpu.VMEM((2, HALF, 2 * HALF), jnp.float32),
            pltpu.VMEM((2, HALF, 2 * HALF), jnp.float32),
            pltpu.VMEM((2, HALF, TILE), jnp.float32),
            pltpu.SemaphoreType.DMA((copies,)),
            pltpu.SemaphoreType.DMA((copies,)),
            pltpu.SemaphoreType.DMA((2, PIECES + 2)),
            pltpu.SemaphoreType.DMA((2, PIECES + 2)),
            pltpu.SemaphoreType.DMA((2, ROW_PIECES)),
            pltpu.SemaphoreType.DMA((2, ROW_PIECES)),
            pltpu.SemaphoreType.DMA((ROW_PIECES,)),
            pltpu.SemaphoreType.DMA((ROW_PIECES,)),
            pltpu.SemaphoreType.DMA((2,)),
            pltpu.SemaphoreType.DMA((2,)),
            pltpu.SemaphoreType.DMA((4,)),
        ],
        compiler_params=pltpu.CompilerParams(collective_id=0, has_side_effects=True, vmem_limit_bytes=VMEM),
        cost_estimate=pl.CostEstimate(flops=M * M * 8, bytes_accessed=100 << 20, transcendentals=0),
        name="send_back",
    )(gleft, gright, gabove, gbelow, gup, gdown, part.reshape(1024, HALF))


def fold_kernel(got_left, got_right, got_up, got_down, tile, out, band, side_band, row_in, strip_in, sems):
    gx, gy = lax.axis_index("gx"), lax.axis_index("gy")
    end = TILE - HALF
    frame = [
        (tile.at[:, pl.ds(0, HALF)], band.at[0]),
        (tile.at[:, pl.ds(end, HALF)], band.at[1]),
        (tile.at[:, pl.ds(HALF, CORE), pl.ds(0, HALF)], side_band.at[0]),
        (tile.at[:, pl.ds(HALF, CORE), pl.ds(end, HALF)], side_band.at[1]),
    ]
    arrived = [(got_up, row_in.at[0]), (got_down, row_in.at[1]), (got_left, strip_in.at[0]), (got_right, strip_in.at[1])]
    loads = start_all(frame + arrived, sems)
    wait_all(loads)
    for i, there in enumerate((gx > 0, gx < 15)):
        @pl.when(there)
        def _():
            band[i] += row_in[i]

    for i, there in enumerate((gy > 0, gy < 7)):
        lanes = slice(end * i, end * i + HALF)

        @pl.when(there)
        def _():
            band[0, :, :, lanes] += strip_in[i, :, :HALF]
            side_band[i] += strip_in[i, :, HALF:end]
            band[1, :, :, lanes] += strip_in[i, :, end:]

    back = [
        (band.at[0], out.at[:, pl.ds(0, HALF)]),
        (band.at[1], out.at[:, pl.ds(end, HALF)]),
        (side_band.at[0], out.at[:, pl.ds(HALF, CORE), pl.ds(0, HALF)]),
        (side_band.at[1], out.at[:, pl.ds(HALF, CORE), pl.ds(end, HALF)]),
    ]
    wait_all(start_all(back, sems))


def fold(tile, got_left, got_right, got_up, got_down):
    return pl.pallas_call(
        fold_kernel,
        out_shape=shaped(2, TILE, TILE),
        in_specs=[HBM_SPEC] * 5,
        out_specs=HBM_SPEC,
        scratch_shapes=[
            pltpu.VMEM((2, 2, HALF, TILE), jnp.float32),
            pltpu.VMEM((2, 2, CORE, HALF), jnp.float32),
            pltpu.VMEM((2, 2, HALF, TILE), jnp.float32),
            pltpu.VMEM((2, 2, TILE, HALF), jnp.float32),
            pltpu.SemaphoreType.DMA((8,)),
        ],
        input_output_aliases={4: 0},
        compiler_params=pltpu.CompilerParams(vmem_limit_bytes=VMEM),
        name="fold",
    )(got_left, got_right, got_up, got_down, tile)


def shift_by_one(x, axis, forward):
    count = lax.axis_size(axis)
    steps = [(i, i + 1) if forward else (i + 1, i) for i in range(count - 1)]
    return lax.ppermute(x, axis, steps)


def to_right(x):
    return shift_by_one(x, "gy", True)


def to_left(x):
    return shift_by_one(x, "gy", False)


def to_down(x):
    return shift_by_one(x, "gx", True)


def to_up(x):
    return shift_by_one(x, "gx", False)


def joint(x, pairs):
    return lax.ppermute(x, ("gx", "gy"), [(8 * a + b, 8 * c + d) for (a, b), (c, d) in pairs])


def crossing_first(x):
    return joint(
        x, [((8, 2 * y), (7, 2 * y + 1)) for y in range(4)] + [((8, 2 * y + 1), (8, 2 * y)) for y in range(4)]
    )


def crossing_second(x):
    return joint(x, [((7, 2 * y + 1), (7, 2 * y)) for y in range(4)] + [((8, 2 * y), (7, 2 * y + 1)) for y in range(4)])


def to_up_straight(x):
    return lax.ppermute(x, "gx", [(i + 1, i) for i in range(15) if i != 7])


def on_device(field, probe, centers, live, measured):
    tables = tuple(jnp.asarray(t) for t in host_tables())
    last, first, later = lax.optimization_barrier((field[:, :, TILE - HALF :], field[:, :, :HALF], field))
    left, right = to_right(last), to_left(first)
    top_rows = later[:, :HALF]
    relayed, up, straight = crossing_first(top_rows), to_down(later[:, TILE - HALF :]), to_up_straight(top_rows)
    grad, acc, losses = inner_slots(centers, live, probe, tables, field, measured)
    relayed, acc = lax.optimization_barrier((relayed, acc))
    second = crossing_second(relayed)
    left, right, up, straight, acc = lax.optimization_barrier((left, right, up, straight, acc))
    above = to_down(jnp.concatenate([left[:, TILE - HALF :], right[:, TILE - HALF :]], axis=2))
    below = to_up(jnp.concatenate([left[:, :HALF], right[:, :HALF]], axis=2))
    down = straight + second
    halos = (left, right, above, below)
    partial = (grad, acc, losses)
    grad, acc, losses, gup, gdown, gleft, gright, gabove, gbelow = outer_slots(
        centers, live, probe, tables, field, up, down, measured, halos, partial
    )
    slots_all = SLOTS_HERE * lax.axis_size("gx") * lax.axis_size("gy")
    *got, probe_grad = send_back(gleft, gright, gabove, gbelow, gup, gdown, acc, 1.0 / math.sqrt(slots_all))
    return fold(grad, *got), probe_grad, losses


def solution(mesh):
    placed = (
        P(None, "gx", "gy"),
        P(),
        P(("gx", "gy"), None),
        P(("gx", "gy")),
        P(("gx", "gy"), None, None),
    )
    return jax.shard_map(
        on_device,
        mesh=mesh,
        in_specs=placed,
        out_specs=(P(None, "gx", "gy"), P(), P(("gx", "gy"))),
        check_vma=False,
    )
```

```python
import functools
import math

import jax
import jax.numpy as jnp
import ml_dtypes
import numpy as np
from jax import lax
from jax.experimental import pallas as pl
from jax.experimental.pallas import tpu as pltpu
from jax.sharding import PartitionSpec as P

M = 256
HALF = 128
TILE = 1024
SLOTS_HERE = 16
ROWS = TILE + 2 * HALF
VMEM = 60 * 1024 * 1024


def split_host(table):
    high = table.astype(ml_dtypes.bfloat16)
    low = (table - high.astype(np.float64)).astype(ml_dtypes.bfloat16)
    return high, low


def host_tables():
    n = np.arange(HALF)
    lefts, rights = [], []
    for odd in (0, 1):
        k = 2 * np.arange(HALF) + odd
        angle = 2.0 * np.pi * (np.outer(k, n) % M) / M
        c, s = np.cos(angle) / 16.0, np.sin(angle) / 16.0
        both = np.block([[c, s], [-s, c]])
        for table in (both, both.T):
            high, low = split_host(table)
            lefts.append(np.concatenate([high, low, high], axis=1))
            rights.append(np.concatenate([high, high, low], axis=0))
    pick = np.zeros((M, M))
    pick[2 * n, n] = 1.0
    pick[2 * n + 1, HALF + n] = 1.0
    pick = pick.astype(ml_dtypes.bfloat16)
    return np.stack(lefts), np.stack(rights), np.concatenate([pick, pick], axis=0)


def halves(x):
    high = x.astype(jnp.bfloat16)
    low = (x - high.astype(jnp.float32)).astype(jnp.bfloat16)
    return high, low


def left_product(table, x):
    high, low = halves(x)
    return jnp.dot(table, jnp.concatenate([high, high, low], axis=0), preferred_element_type=jnp.float32)


def right_product(x, table):
    high, low = halves(x)
    return jnp.dot(jnp.concatenate([high, low, high], axis=1), table, preferred_element_type=jnp.float32)


def visit(obj, grad, probe, seen, slot, lefts, rights, pick, acc, row, block, block_end, shift, ready=None):
    lane = lax.broadcasted_iota(jnp.int32, (M, HALF), 1)
    wraps = lane < shift
    rows = pl.ds(row, M)

    def window(part):
        first = jnp.where(wraps, obj[part, block_end, rows, :], obj[part, block, rows, :])
        return jnp.concatenate([first, obj[part, block + 1, rows, :]], axis=1)

    obj_re, obj_im = window(0), window(1)
    probe_re = pltpu.roll(probe[0], shift, 1)
    probe_im = pltpu.roll(probe[1], shift, 1)
    wave_re = probe_re * obj_re - probe_im * obj_im
    wave_im = probe_re * obj_im + probe_im * obj_re
    top, low = slice(0, HALF), slice(HALF, M)
    yield None
    even = left_product(lefts[0], jnp.concatenate([wave_re[top] + wave_re[low], wave_im[top] + wave_im[low]], axis=0))
    odd = left_product(lefts[2], jnp.concatenate([wave_re[top] - wave_re[low], wave_im[top] - wave_im[low]], axis=0))
    yield None
    half_re = jnp.concatenate([even[top], odd[top]], axis=0)
    half_im = jnp.concatenate([even[low], odd[low]], axis=0)
    far_e = right_product(
        jnp.concatenate([half_re[:, top] + half_re[:, low], half_im[:, top] + half_im[:, low]], axis=1), rights[1]
    )
    far_o = right_product(
        jnp.concatenate([half_re[:, top] - half_re[:, low], half_im[:, top] - half_im[:, low]], axis=1), rights[3]
    )
    yield None
    meas = jnp.concatenate(
        [
            jnp.concatenate([seen[slot, side, pl.ds(odd, HALF, stride=2), :] for side in range(2)], axis=1)
            for odd in range(2)
        ],
        axis=0,
    )
    meas = jnp.dot(jnp.concatenate(halves(meas), axis=1), pick[...], preferred_element_type=jnp.float32)

    def residual(far, seen):
        squares = far * far
        total = squares[:, top] + squares[:, low] + 1.0
        inverse = lax.rsqrt(total)
        differ = total * inverse - seen
        factor = differ * inverse
        return far * jnp.concatenate([factor, factor], axis=1), differ * differ

    back_e, loss_e = residual(far_e, meas[:, top])
    back_o, loss_o = residual(far_o, meas[:, low])
    loss = jnp.sum(loss_e + loss_o) * (0.5 / (M * M))
    yield None
    up = right_product(back_e, rights[0])
    vp = right_product(back_o, rights[2])
    yield None
    plus, minus = up + vp, up - vp
    half_re = jnp.concatenate([plus[:, top], minus[:, top]], axis=1)
    half_im = jnp.concatenate([plus[:, low], minus[:, low]], axis=1)
    up = left_product(lefts[1], jnp.concatenate([half_re[top], half_im[top]], axis=0))
    vp = left_product(lefts[3], jnp.concatenate([half_re[low], half_im[low]], axis=0))
    yield None
    plus, minus = up + vp, up - vp
    back_re = jnp.concatenate([plus[top], minus[top]], axis=0)
    back_im = jnp.concatenate([plus[low], minus[low]], axis=0)

    grads = (probe_re * back_re + probe_im * back_im, probe_re * back_im - probe_im * back_re)
    yield None
    if ready is not None:
        ready()
    for part, g in enumerate(grads):
        first = g[:, top]
        grad[part, block, rows, :] += jnp.where(wraps, 0.0, first)
        grad[part, block + 1, rows, :] += g[:, low]
        grad[part, block_end, rows, :] += jnp.where(wraps, first, 0.0)
    unshift = lax.rem(M - shift, M)
    terms = (obj_re * back_re + obj_im * back_im, obj_re * back_im - obj_im * back_re)
    for part, term in enumerate(terms):
        turned = pltpu.roll(term, unshift, 1)
        acc[part, 0] += turned[:, top]
        acc[part, 1] += turned[:, low]
    yield loss


INNER_COST = SLOTS_HERE
CORE = TILE - 2 * HALF


def start_all(pairs, sems):
    copies = [pltpu.make_async_copy(source, target, sems.at[i]) for i, (source, target) in enumerate(pairs)]
    for copy in copies:
        copy.start()
    return copies


def wait_all(copies):
    for copy in copies:
        copy.wait()


def block_of(ref, index):
    return ref.at[:, :, pl.ds(HALF * index, HALF)]


def inner_pairs(tile, buffer, slots, first_row):
    return [(block_of(tile, block), buffer.at[:, place, pl.ds(first_row, TILE)]) for place, block in slots]


def border_pairs(tile, buffer, slots):
    pairs = []
    for place, block in slots:
        spans = ((0, TILE),) if block in (0, 1, 6, 7) else ((0, 2 * HALF), (TILE - 2 * HALF, 2 * HALF))
        for at, size in spans:
            pairs.append(
                (tile.at[:, pl.ds(at, size), pl.ds(HALF * block, HALF)], buffer.at[:, place, pl.ds(HALF + at, size)])
            )
    return pairs


def band_pairs(up, down, buffer, slots):
    pairs = []
    for place, block in slots:
        pairs.append((block_of(up, block), buffer.at[:, place, pl.ds(0, HALF)]))
        pairs.append((block_of(down, block), buffer.at[:, place, pl.ds(HALF + TILE, HALF)]))
    return pairs


def strip_pairs(strip, above, below, side, buffer, place):
    return [
        (strip, buffer.at[:, place, pl.ds(HALF, TILE)]),
        (block_of(above, side), buffer.at[:, place, pl.ds(0, HALF)]),
        (block_of(below, side), buffer.at[:, place, pl.ds(HALF + TILE, HALF)]),
    ]


def flipped(pairs):
    return [(target, source) for source, target in pairs]


def slot_copies(measured, seen, slot_sems, s):
    return [
        pltpu.make_async_copy(measured.at[s, :, pl.ds(HALF * side, HALF)], seen.at[s, side], slot_sems.at[s, side])
        for side in range(2)
    ]


def fetch_slots(live, centers, wanted, measured, seen, slot_sems, order):
    order[SLOTS_HERE] = 0

    def fetch(s, carry):
        @pl.when(wanted(live[s], centers[s, 0], centers[s, 1]))
        def _():
            for copy in slot_copies(measured, seen, slot_sems, s):
                copy.start()
            count = order[SLOTS_HERE]
            order[count] = s
            order[SLOTS_HERE] = count + 1

        return carry

    lax.fori_loop(0, SLOTS_HERE, fetch, 0)


def run_slots(centers, offset, blocks, measured, seen, slot_sems, order, losses, body):
    def together(first, size):
        chosen = [order[first + i] for i in range(size)]
        for s in chosen:
            wait_all(slot_copies(measured, seen, slot_sems, s))
        runs = []
        for i, s in enumerate(chosen):
            row, column = centers[s, 0] - offset, centers[s, 1] - offset
            block = lax.div(column, HALF)
            runs.append(body(i, s, row, block, jnp.minimum(block + 2, blocks - 1), lax.rem(column, HALF)))
        finished = 0
        while finished < size:
            for s, run in zip(chosen, runs):
                loss = next(run)
                if loss is not None:
                    losses[s] = loss
                    finished += 1

    count = order[SLOTS_HERE]
    pairs = lax.div(count, 2)

    def step(p, carry):
        together(2 * p, 2)
        return carry

    lax.fori_loop(0, pairs, step, 0)

    @pl.when(count > 2 * pairs)
    def _():
        together(count - 1, 1)


def within(row, column):
    return (row >= HALF) & (row <= TILE - HALF) & (column >= HALF) & (column <= TILE - HALF)


def is_inner(alive, row, column):
    return (alive > 0) & within(row, column)


def is_outer(alive, row, column):
    return (alive > 0) & jnp.logical_not(within(row, column))


def inner_kernel(
    centers, live, probe, lefts, rights, pick, field, measured, grad_out, acc, losses, obj, grad, seen, sems, slot_sems, order
):
    slots = [(j, j) for j in range(8)]
    loads = start_all(inner_pairs(field, obj, slots, 0), sems)
    fetch_slots(live, centers, is_inner, measured, seen, slot_sems, order)
    grad[...] = jnp.zeros_like(grad)
    acc[...] = jnp.zeros_like(acc)
    for s in range(SLOTS_HERE):
        losses[s] = 0.0
    wait_all(loads)

    def body(i, s, row, block, block_end, shift):
        return visit(obj, grad, probe, seen, s, lefts, rights, pick, acc, row, block, block_end, shift)

    run_slots(centers, HALF, 8, measured, seen, slot_sems, order, losses, body)
    wait_all(start_all(flipped(inner_pairs(grad_out, grad, slots, 0)), sems))


def outer_kernel(
    centers, live, probe, lefts, rights, pick, field, up, down, measured,
    left, right, above, below, grad_in, acc_in, losses_in,
    grad_out, acc, losses, up_out, down_out, gleft, gright, gabove, gbelow,
    obj, grad, seen, sems, slot_sems, order, grad_sems, loaded,
):
    slots = [(j + 1, j) for j in range(8)]
    loads = start_all(
        border_pairs(field, obj, slots)
        + band_pairs(up, down, obj, slots)
        + strip_pairs(left, above, below, 0, obj, 0)
        + strip_pairs(right, above, below, 1, obj, 9),
        sems,
    )
    fetch_slots(live, centers, is_outer, measured, seen, slot_sems, order)
    grad_loads = start_all(border_pairs(grad_in, grad, slots), grad_sems)
    for place_at in (0, 9):
        grad[:, place_at] = jnp.zeros((2, ROWS, HALF), jnp.float32)
    for row_at in (0, HALF + TILE):
        grad[:, 1:9, row_at : row_at + HALF] = jnp.zeros((2, 8, HALF, HALF), jnp.float32)
    acc[...] = acc_in[...]
    for s in range(SLOTS_HERE):
        losses[s] = losses_in[s]
    wait_all(loads)
    loaded[0] = 0

    def have_grads():
        @pl.when(loaded[0] == 0)
        def _():
            wait_all(grad_loads)
            loaded[0] = 1

    def body(i, s, row, block, block_end, shift):
        return visit(obj, grad, probe, seen, s, lefts, rights, pick, acc, row, block, block_end, shift, None if i else have_grads)

    run_slots(centers, 0, 10, measured, seen, slot_sems, order, losses, body)
    have_grads()
    wait_all(
        start_all(
            flipped(
                strip_pairs(gleft, gabove, gbelow, 0, grad, 0)
                + strip_pairs(gright, gabove, gbelow, 1, grad, 9)
                + band_pairs(up_out, down_out, grad, slots)
                + border_pairs(grad_out, grad, slots)
            ),
            sems,
        )
    )


VMEM_SPEC = pl.BlockSpec(memory_space=pltpu.VMEM)
SMEM_SPEC = pl.BlockSpec(memory_space=pltpu.SMEM)
HBM_SPEC = pl.BlockSpec(memory_space=pl.ANY)


def shaped(*shape):
    return jax.ShapeDtypeStruct(shape, jnp.float32)


def slot_scratch(blocks, copies):
    return [
        pltpu.VMEM((2, blocks, HALF * blocks, HALF), jnp.float32),
        pltpu.VMEM((2, blocks, HALF * blocks, HALF), jnp.float32),
        pltpu.VMEM((SLOTS_HERE, 2, M, HALF), jnp.float32),
        pltpu.SemaphoreType.DMA((copies,)),
        pltpu.SemaphoreType.DMA((SLOTS_HERE, 2)),
        pltpu.SMEM((SLOTS_HERE + 1,), jnp.int32),
    ]


def cost(slots):
    return pl.CostEstimate(flops=slots * 26 * 2 * M**3, bytes_accessed=30 << 20, transcendentals=slots * M * M)


TILE_OUT = (shaped(2, TILE, TILE), shaped(2, 2, M, HALF), shaped(SLOTS_HERE))
TILE_SPECS = (HBM_SPEC, VMEM_SPEC, SMEM_SPEC)


def inner_slots(centers, live, probe, tables, field, measured):
    return pl.pallas_call(
        inner_kernel,
        out_shape=TILE_OUT,
        in_specs=[SMEM_SPEC] * 2 + [VMEM_SPEC] * 4 + [HBM_SPEC] * 2,
        out_specs=TILE_SPECS,
        scratch_shapes=slot_scratch(8, 8),
        compiler_params=pltpu.CompilerParams(vmem_limit_bytes=VMEM),
        cost_estimate=cost(INNER_COST),
        name="inner_slots",
    )(centers, live, probe, *tables, field, measured)


def outer_slots(centers, live, probe, tables, field, up, down, measured, halos, partial):
    return pl.pallas_call(
        outer_kernel,
        out_shape=TILE_OUT + (shaped(2, HALF, TILE),) * 2 + (shaped(2, TILE, HALF),) * 2 + (shaped(2, HALF, 2 * HALF),) * 2,
        in_specs=[SMEM_SPEC] * 2 + [VMEM_SPEC] * 4 + [HBM_SPEC] * 9 + [VMEM_SPEC, SMEM_SPEC],
        out_specs=TILE_SPECS + (HBM_SPEC,) * 6,
        scratch_shapes=slot_scratch(10, 34) + [pltpu.SemaphoreType.DMA((12,)), pltpu.SMEM((1,), jnp.int32)],
        input_output_aliases={14: 0},
        compiler_params=pltpu.CompilerParams(vmem_limit_bytes=VMEM),
        cost_estimate=cost(SLOTS_HERE // 2),
        name="outer_slots",
    )(centers, live, probe, *tables, field, up, down, measured, *halos, *partial)


MESH = pl.DeviceIdType.MESH
SHARE = 8
PIECES = CORE // HALF
ROW_PIECES = 4
ROW_STEP = HALF // ROW_PIECES


def return_kernel(
    scale, gleft, gright, gabove, gbelow, gup, gdown, part,
    got_left, got_right, got_up, got_down, out,
    first, second, third, kept1, kept2, kept3, full, edges, from_up, from_down, relay,
    sum_send, sum_recv, strip_send, strip_recv, row_send, row_recv, relay_send, relay_recv, corner_send, corner_recv, local,
):
    gx, gy = lax.axis_index("gx"), lax.axis_index("gy")
    core = lax.rem(gx, 2)
    spot = lax.rem(lax.div(gx, 2), 4)
    upper = lax.div(gx, 8)
    group = upper * 8 + gy
    odd = lax.rem(gy, 2)
    has_up, has_down, has_left, has_right = gx > 0, gx < 15, gy > 0, gy < 7
    crosses = gx == 8
    relays = ((gx == 7) & (odd == 1)) | ((gx == 8) & (odd == 0))
    cross_target = (jnp.where(odd == 0, 7, 8), jnp.where(odd == 0, gy + 1, gy - 1))
    relay_target = (7, jnp.where(gx == 7, gy - 1, gy + 1))
    up, down, left, right = (gx - 1, gy), (gx + 1, gy), (gx, gy - 1), (gx, gy + 1)
    far_pair = (15 - gx, jnp.where(gx == 7, gy - 1, gy + 1))

    def at_spot(k):
        return (gx + 2 * (k - spot), gy)

    def at_group(k):
        return (gx + 8 * (lax.div(k, 8) - upper), lax.rem(k, 8))

    other = (gx + 1 - 2 * core, gy)
    spots = [lax.rem(spot + d, 4) for d in range(1, 4)]
    groups = [lax.rem(group + d, 16) for d in range(1, 16)]
    barrier = pltpu.get_barrier_semaphore()

    def greet(device):
        pl.semaphore_signal(barrier, inc=1, device_id=device, device_id_type=MESH)

    sides = ((has_up, up), (has_down, down), (has_left, left), (has_right, right), (relays, far_pair))
    for there, device in sides:
        pl.when(there)(functools.partial(greet, device))
    always = [other] + [at_spot(k) for k in spots] + [at_group(k) for k in groups]
    for device in always:
        greet(device)
    expected = len(always)
    for there, _ in sides:
        expected = expected + there.astype(jnp.int32)
    pl.semaphore_wait(barrier, expected)

    def remote(source, target, send_sem, recv_sem, device):
        return pltpu.make_async_remote_copy(
            src_ref=source, dst_ref=target, send_sem=send_sem, recv_sem=recv_sem, device_id=device, device_id_type=MESH
        )

    corner_up = remote(gabove, from_down, corner_send.at[0], corner_recv.at[0], up)
    corner_down = remote(gbelow, from_up, corner_send.at[1], corner_recv.at[1], down)
    pl.when(has_up)(corner_up.start)
    pl.when(has_down)(corner_down.start)
    strips = (gleft, gright)
    loads = [
        pltpu.make_async_copy(strips[side].at[:, pl.ds(at, HALF)], edges.at[side, :, pl.ds(to, HALF)], local.at[2 * side + i])
        for side in range(2)
        for i, (at, to) in enumerate(((0, 0), (TILE - HALF, HALF)))
    ]
    for copy in loads:
        copy.start()

    def strip_copy(side, piece):
        if piece < PIECES:
            source = strips[side].at[:, pl.ds(HALF * (piece + 1), HALF)]
            place = HALF * (piece + 1)
        else:
            end = piece - PIECES
            source = edges.at[side, :, pl.ds(HALF * end, HALF)]
            place = (TILE - HALF) * end
        target = (got_right, got_left)[side].at[:, pl.ds(place, HALF)]
        return remote(source, target, strip_send.at[side, piece], strip_recv.at[side, piece], (left, right)[side])

    def strip_start(piece):
        pl.when(has_left)(lambda: strip_copy(0, piece).start())
        pl.when(has_right)(lambda: strip_copy(1, piece).start())

    def strip_sent(piece):
        pl.when(has_left)(lambda: strip_copy(0, piece).wait_send())
        pl.when(has_right)(lambda: strip_copy(1, piece).wait_send())

    def strip_got(piece):
        pl.when(has_right)(lambda: strip_copy(0, piece).wait_recv())
        pl.when(has_left)(lambda: strip_copy(1, piece).wait_recv())

    def row_rows(piece):
        return pl.ds(ROW_STEP * piece, ROW_STEP)

    def row_up(piece, direct):
        source = gup.at[:, row_rows(piece)]
        if direct:
            return remote(source, got_down.at[:, row_rows(piece)], row_send.at[0, piece], row_recv.at[0, piece], up)
        return remote(source, relay.at[:, row_rows(piece)], row_send.at[0, piece], relay_recv.at[piece], cross_target)

    def row_forward(piece):
        return remote(
            relay.at[:, row_rows(piece)], got_down.at[:, row_rows(piece)], relay_send.at[piece], row_recv.at[0, piece], relay_target
        )

    def row_down(piece):
        rows = row_rows(piece)
        return remote(gdown.at[:, rows], got_up.at[:, rows], row_send.at[1, piece], row_recv.at[1, piece], down)

    straight = has_up & (gx != 8)

    def row_start(piece):
        pl.when(straight)(lambda: row_up(piece, True).start())
        pl.when(crosses)(lambda: row_up(piece, False).start())
        pl.when(has_down)(lambda: row_down(piece).start())

    def relay_on(piece):
        def go():
            row_up(piece, False).wait_recv()
            row_forward(piece).start()

        pl.when(relays)(go)

    def rows(start, size):
        return pl.ds(pl.multiple_of(start, 8), size)

    count = [0]

    def send(source, target, device):
        i = count[0]
        count[0] += 1
        copy = remote(source, target, sum_send.at[i], sum_recv.at[i], device)
        copy.start()
        return copy

    def arrive(copies):
        for copy in copies:
            copy.wait_recv()

    strip_start(0)
    stage = [send(part.at[rows((1 - core) * 512, 512)], first, other)]
    sent = list(stage)
    row_start(0)
    strip_start(1)
    arrive(stage)
    kept1[...] = part[rows(core * 512, 512), :] + first[...]
    stage = [send(kept1.at[rows(k * 128, 128)], second.at[d], at_spot(k)) for d, k in enumerate(spots)]
    sent += stage
    for copy in loads:
        copy.wait()

    @pl.when(has_down)
    def _():
        corner_up.wait_recv()
        for side in range(2):
            edges[side, :, HALF:] += from_down[:, :, HALF * side : HALF * (side + 1)]

    @pl.when(has_up)
    def _():
        corner_down.wait_recv()
        for side in range(2):
            edges[side, :, :HALF] += from_up[:, :, HALF * side : HALF * (side + 1)]

    row_start(1)
    strip_start(2)
    strip_sent(0)
    arrive(stage)
    kept2[...] = kept1[rows(spot * 128, 128), :] + (second[0] + second[1] + second[2])
    stage = [send(kept2.at[rows(k * SHARE, SHARE)], third.at[d], at_group(k)) for d, k in enumerate(groups)]
    sent += stage
    relay_on(0)
    row_start(2)
    strip_start(3)
    strip_sent(1)
    arrive(stage)
    total = kept2[rows(group * SHARE, SHARE), :]
    for d in range(15):
        total = total + third[d]
    kept3[...] = total * scale
    mine = rows(core * 512 + spot * 128 + group * SHARE, SHARE)
    full[mine, :] = kept3[...]
    stage = [send(kept3, full.at[mine], at_group(k)) for k in groups]
    sent += stage
    relay_on(1)
    row_start(3)
    strip_start(4)
    strip_sent(2)
    arrive(stage)
    quarter = full.at[rows(core * 512 + spot * 128, 128)]
    stage = [send(quarter, quarter, at_spot(k)) for k in spots]
    sent += stage
    relay_on(2)
    strip_start(5)
    strip_sent(3)
    arrive(stage)
    whole = full.at[rows(core * 512, 512)]
    stage = [send(whole, whole, other)]
    sent += stage
    relay_on(3)
    strip_start(6)
    strip_start(7)
    arrive(stage)
    for part_at in range(2):
        for side in range(2):
            out[part_at, :, HALF * side : HALF * (side + 1)] = full[pl.ds((part_at * 2 + side) * M, M), :]
    for piece in range(4, PIECES + 2):
        strip_sent(piece)
    for piece in range(PIECES + 2):
        strip_got(piece)
    for piece in range(ROW_PIECES):
        pl.when(has_down)(lambda: row_down(piece).wait_send())
        pl.when(has_up)(lambda: row_up(piece, True).wait_send())
        pl.when(relays)(lambda: row_forward(piece).wait_send())
        pl.when(has_down)(lambda: row_up(piece, True).wait_recv())
        pl.when(has_up)(lambda: row_down(piece).wait_recv())
    pl.when(has_up)(corner_up.wait_send)
    pl.when(has_down)(corner_down.wait_send)
    for copy in sent:
        copy.wait_send()


def send_back(gleft, gright, gabove, gbelow, gup, gdown, part, scale):
    copies = 2 * (1 + 3 + 15)
    return pl.pallas_call(
        functools.partial(return_kernel, scale),
        out_shape=(shaped(2, TILE, HALF),) * 2 + (shaped(2, HALF, TILE),) * 2 + (shaped(2, M, M),),
        in_specs=[HBM_SPEC] * 6 + [VMEM_SPEC],
        out_specs=(HBM_SPEC,) * 4 + (VMEM_SPEC,),
        scratch_shapes=[
            pltpu.VMEM((512, HALF), jnp.float32),
            pltpu.VMEM((3, 128, HALF), jnp.float32),
            pltpu.VMEM((15, SHARE, HALF), jnp.float32),
            pltpu.VMEM((512, HALF), jnp.float32),
            pltpu.VMEM((128, HALF), jnp.float32),
            pltpu.VMEM((SHARE, HALF), jnp.float32),
            pltpu.VMEM((1024, HALF), jnp.float32),
            pltpu.VMEM((2, 2, 2 * HALF, HALF), jnp.float32),
            pltpu.VMEM((2, HALF, 2 * HALF), jnp.float32),
            pltpu.VMEM((2, HALF, 2 * HALF), jnp.float32),
            pltpu.VMEM((2, HALF, TILE), jnp.float32),
            pltpu.SemaphoreType.DMA((copies,)),
            pltpu.SemaphoreType.DMA((copies,)),
            pltpu.SemaphoreType.DMA((2, PIECES + 2)),
            pltpu.SemaphoreType.DMA((2, PIECES + 2)),
            pltpu.SemaphoreType.DMA((2, ROW_PIECES)),
            pltpu.SemaphoreType.DMA((2, ROW_PIECES)),
            pltpu.SemaphoreType.DMA((ROW_PIECES,)),
            pltpu.SemaphoreType.DMA((ROW_PIECES,)),
            pltpu.SemaphoreType.DMA((2,)),
            pltpu.SemaphoreType.DMA((2,)),
            pltpu.SemaphoreType.DMA((4,)),
        ],
        compiler_params=pltpu.CompilerParams(collective_id=0, has_side_effects=True, vmem_limit_bytes=VMEM),
        cost_estimate=pl.CostEstimate(flops=M * M * 8, bytes_accessed=100 << 20, transcendentals=0),
        name="send_back",
    )(gleft, gright, gabove, gbelow, gup, gdown, part.reshape(1024, HALF))


def fold_kernel(got_left, got_right, got_up, got_down, tile, out, band, side_band, row_in, strip_in, sems):
    gx, gy = lax.axis_index("gx"), lax.axis_index("gy")
    end = TILE - HALF
    frame = [
        (tile.at[:, pl.ds(0, HALF)], band.at[0]),
        (tile.at[:, pl.ds(end, HALF)], band.at[1]),
        (tile.at[:, pl.ds(HALF, CORE), pl.ds(0, HALF)], side_band.at[0]),
        (tile.at[:, pl.ds(HALF, CORE), pl.ds(end, HALF)], side_band.at[1]),
    ]
    arrived = [(got_up, row_in.at[0]), (got_down, row_in.at[1]), (got_left, strip_in.at[0]), (got_right, strip_in.at[1])]
    loads = start_all(frame + arrived, sems)
    wait_all(loads)
    for i, there in enumerate((gx > 0, gx < 15)):
        @pl.when(there)
        def _():
            band[i] += row_in[i]

    for i, there in enumerate((gy > 0, gy < 7)):
        lanes = slice(end * i, end * i + HALF)

        @pl.when(there)
        def _():
            band[0, :, :, lanes] += strip_in[i, :, :HALF]
            side_band[i] += strip_in[i, :, HALF:end]
            band[1, :, :, lanes] += strip_in[i, :, end:]

    back = [
        (band.at[0], out.at[:, pl.ds(0, HALF)]),
        (band.at[1], out.at[:, pl.ds(end, HALF)]),
        (side_band.at[0], out.at[:, pl.ds(HALF, CORE), pl.ds(0, HALF)]),
        (side_band.at[1], out.at[:, pl.ds(HALF, CORE), pl.ds(end, HALF)]),
    ]
    wait_all(start_all(back, sems))


def fold(tile, got_left, got_right, got_up, got_down):
    return pl.pallas_call(
        fold_kernel,
        out_shape=shaped(2, TILE, TILE),
        in_specs=[HBM_SPEC] * 5,
        out_specs=HBM_SPEC,
        scratch_shapes=[
            pltpu.VMEM((2, 2, HALF, TILE), jnp.float32),
            pltpu.VMEM((2, 2, CORE, HALF), jnp.float32),
            pltpu.VMEM((2, 2, HALF, TILE), jnp.float32),
            pltpu.VMEM((2, 2, TILE, HALF), jnp.float32),
            pltpu.SemaphoreType.DMA((8,)),
        ],
        input_output_aliases={4: 0},
        compiler_params=pltpu.CompilerParams(vmem_limit_bytes=VMEM),
        name="fold",
    )(got_left, got_right, got_up, got_down, tile)


def shift_by_one(x, axis, forward):
    count = lax.axis_size(axis)
    steps = [(i, i + 1) if forward else (i + 1, i) for i in range(count - 1)]
    return lax.ppermute(x, axis, steps)


def to_right(x):
    return shift_by_one(x, "gy", True)


def to_left(x):
    return shift_by_one(x, "gy", False)


def to_down(x):
    return shift_by_one(x, "gx", True)


def to_up(x):
    return shift_by_one(x, "gx", False)


def joint(x, pairs):
    return lax.ppermute(x, ("gx", "gy"), [(8 * a + b, 8 * c + d) for (a, b), (c, d) in pairs])


def crossing_first(x):
    return joint(
        x, [((8, 2 * y), (7, 2 * y + 1)) for y in range(4)] + [((8, 2 * y + 1), (8, 2 * y)) for y in range(4)]
    )


def crossing_second(x):
    return joint(x, [((7, 2 * y + 1), (7, 2 * y)) for y in range(4)] + [((8, 2 * y), (7, 2 * y + 1)) for y in range(4)])


def to_up_straight(x):
    return lax.ppermute(x, "gx", [(i + 1, i) for i in range(15) if i != 7])


def on_device(field, probe, centers, live, measured):
    tables = tuple(jnp.asarray(t) for t in host_tables())
    last, first, later = lax.optimization_barrier((field[:, :, TILE - HALF :], field[:, :, :HALF], field))
    left, right = to_right(last), to_left(first)
    top_rows = later[:, :HALF]
    relayed, up, straight = crossing_first(top_rows), to_down(later[:, TILE - HALF :]), to_up_straight(top_rows)
    grad, acc, losses = inner_slots(centers, live, probe, tables, field, measured)
    relayed, acc = lax.optimization_barrier((relayed, acc))
    second = crossing_second(relayed)
    left, right, up, straight, acc = lax.optimization_barrier((left, right, up, straight, acc))
    above = to_down(jnp.concatenate([left[:, TILE - HALF :], right[:, TILE - HALF :]], axis=2))
    below = to_up(jnp.concatenate([left[:, :HALF], right[:, :HALF]], axis=2))
    down = straight + second
    halos = (left, right, above, below)
    partial = (grad, acc, losses)
    grad, acc, losses, gup, gdown, gleft, gright, gabove, gbelow = outer_slots(
        centers, live, probe, tables, field, up, down, measured, halos, partial
    )
    slots_all = SLOTS_HERE * lax.axis_size("gx") * lax.axis_size("gy")
    *got, probe_grad = send_back(gleft, gright, gabove, gbelow, gup, gdown, acc, 1.0 / math.sqrt(slots_all))
    return fold(grad, *got), probe_grad, losses


def solution(mesh):
    placed = (
        P(None, "gx", "gy"),
        P(),
        P(("gx", "gy"), None),
        P(("gx", "gy")),
        P(("gx", "gy"), None, None),
    )
    return jax.shard_map(
        on_device,
        mesh=mesh,
        in_specs=placed,
        out_specs=(P(None, "gx", "gy"), P(), P(("gx", "gy"))),
        check_vma=False,
    )
```

```python
import functools
import math

import jax
import jax.numpy as jnp
import ml_dtypes
import numpy as np
from jax import lax
from jax.experimental import pallas as pl
from jax.experimental.pallas import tpu as pltpu
from jax.sharding import PartitionSpec as P

M = 256
HALF = 128
TILE = 1024
SLOTS_HERE = 16
ROWS = TILE + 2 * HALF
VMEM = 60 * 1024 * 1024


def split_host(table):
    high = table.astype(ml_dtypes.bfloat16)
    low = (table - high.astype(np.float64)).astype(ml_dtypes.bfloat16)
    return high, low


def host_tables():
    n = np.arange(HALF)
    lefts, rights = [], []
    for odd in (0, 1):
        k = 2 * np.arange(HALF) + odd
        angle = 2.0 * np.pi * (np.outer(k, n) % M) / M
        c, s = np.cos(angle) / 16.0, np.sin(angle) / 16.0
        both = np.block([[c, s], [-s, c]])
        for table in (both, both.T):
            high, low = split_host(table)
            lefts.append(np.concatenate([high, low, high], axis=1))
            rights.append(np.concatenate([high, high, low], axis=0))
    pick = np.zeros((M, M))
    pick[2 * n, n] = 1.0
    pick[2 * n + 1, HALF + n] = 1.0
    pick = pick.astype(ml_dtypes.bfloat16)
    return np.stack(lefts), np.stack(rights), np.concatenate([pick, pick], axis=0)


def halves(x):
    high = x.astype(jnp.bfloat16)
    low = (x - high.astype(jnp.float32)).astype(jnp.bfloat16)
    return high, low


def left_product(table, x):
    high, low = halves(x)
    return jnp.dot(table, jnp.concatenate([high, high, low], axis=0), preferred_element_type=jnp.float32)


def right_product(x, table):
    high, low = halves(x)
    return jnp.dot(jnp.concatenate([high, low, high], axis=1), table, preferred_element_type=jnp.float32)


def visit(obj, grad, probe, seen, slot, lefts, rights, pick, acc, row, block, block_end, shift, ready=None):
    lane = lax.broadcasted_iota(jnp.int32, (M, HALF), 1)
    wraps = lane < shift
    rows = pl.ds(row, M)

    def window(part):
        first = jnp.where(wraps, obj[part, block_end, rows, :], obj[part, block, rows, :])
        return jnp.concatenate([first, obj[part, block + 1, rows, :]], axis=1)

    obj_re, obj_im = window(0), window(1)
    probe_re = pltpu.roll(probe[0], shift, 1)
    probe_im = pltpu.roll(probe[1], shift, 1)
    wave_re = probe_re * obj_re - probe_im * obj_im
    wave_im = probe_re * obj_im + probe_im * obj_re
    top, low = slice(0, HALF), slice(HALF, M)
    yield None
    even = left_product(lefts[0], jnp.concatenate([wave_re[top] + wave_re[low], wave_im[top] + wave_im[low]], axis=0))
    odd = left_product(lefts[2], jnp.concatenate([wave_re[top] - wave_re[low], wave_im[top] - wave_im[low]], axis=0))
    yield None
    half_re = jnp.concatenate([even[top], odd[top]], axis=0)
    half_im = jnp.concatenate([even[low], odd[low]], axis=0)
    far_e = right_product(
        jnp.concatenate([half_re[:, top] + half_re[:, low], half_im[:, top] + half_im[:, low]], axis=1), rights[1]
    )
    far_o = right_product(
        jnp.concatenate([half_re[:, top] - half_re[:, low], half_im[:, top] - half_im[:, low]], axis=1), rights[3]
    )
    yield None
    meas = jnp.concatenate(
        [
            jnp.concatenate([seen[slot, side, pl.ds(odd, HALF, stride=2), :] for side in range(2)], axis=1)
            for odd in range(2)
        ],
        axis=0,
    )
    meas = jnp.dot(jnp.concatenate(halves(meas), axis=1), pick[...], preferred_element_type=jnp.float32)

    def residual(far, seen):
        squares = far * far
        total = squares[:, top] + squares[:, low] + 1.0
        inverse = lax.rsqrt(total)
        differ = total * inverse - seen
        factor = differ * inverse
        return far * jnp.concatenate([factor, factor], axis=1), differ * differ

    back_e, loss_e = residual(far_e, meas[:, top])
    back_o, loss_o = residual(far_o, meas[:, low])
    loss = jnp.sum(loss_e + loss_o) * (0.5 / (M * M))
    yield None
    up = right_product(back_e, rights[0])
    vp = right_product(back_o, rights[2])
    yield None
    plus, minus = up + vp, up - vp
    half_re = jnp.concatenate([plus[:, top], minus[:, top]], axis=1)
    half_im = jnp.concatenate([plus[:, low], minus[:, low]], axis=1)
    up = left_product(lefts[1], jnp.concatenate([half_re[top], half_im[top]], axis=0))
    vp = left_product(lefts[3], jnp.concatenate([half_re[low], half_im[low]], axis=0))
    yield None
    plus, minus = up + vp, up - vp
    back_re = jnp.concatenate([plus[top], minus[top]], axis=0)
    back_im = jnp.concatenate([plus[low], minus[low]], axis=0)

    grads = (probe_re * back_re + probe_im * back_im, probe_re * back_im - probe_im * back_re)
    yield None
    if ready is not None:
        ready()
    for part, g in enumerate(grads):
        first = g[:, top]
        grad[part, block, rows, :] += jnp.where(wraps, 0.0, first)
        grad[part, block + 1, rows, :] += g[:, low]
        grad[part, block_end, rows, :] += jnp.where(wraps, first, 0.0)
    unshift = lax.rem(M - shift, M)
    terms = (obj_re * back_re + obj_im * back_im, obj_re * back_im - obj_im * back_re)
    for part, term in enumerate(terms):
        turned = pltpu.roll(term, unshift, 1)
        acc[part, 0] += turned[:, top]
        acc[part, 1] += turned[:, low]
    yield loss


INNER_COST = SLOTS_HERE
CORE = TILE - 2 * HALF


def start_all(pairs, sems):
    copies = [pltpu.make_async_copy(source, target, sems.at[i]) for i, (source, target) in enumerate(pairs)]
    for copy in copies:
        copy.start()
    return copies


def start_only(pairs, sems):
    start_all(pairs, sems)


def wait_all(copies):
    for copy in copies:
        copy.wait()


def block_of(ref, index):
    return ref.at[:, :, pl.ds(HALF * index, HALF)]


def inner_pairs(tile, buffer, slots, first_row):
    return [(block_of(tile, block), buffer.at[:, place, pl.ds(first_row, TILE)]) for place, block in slots]


def border_pairs(tile, buffer, slots):
    pairs = []
    for place, block in slots:
        spans = ((0, TILE),) if block in (0, 1, 6, 7) else ((0, 2 * HALF), (TILE - 2 * HALF, 2 * HALF))
        for at, size in spans:
            pairs.append(
                (tile.at[:, pl.ds(at, size), pl.ds(HALF * block, HALF)], buffer.at[:, place, pl.ds(HALF + at, size)])
            )
    return pairs


def row_pairs(rows, first_row, buffer, slots):
    return [(block_of(rows, block), buffer.at[:, place, pl.ds(first_row, HALF)]) for place, block in slots]


def band_pairs(up, down, buffer, slots):
    return row_pairs(up, 0, buffer, slots) + row_pairs(down, HALF + TILE, buffer, slots)


def strip_pairs(strip, above, below, side, buffer, place):
    return [
        (strip, buffer.at[:, place, pl.ds(HALF, TILE)]),
        (block_of(above, side), buffer.at[:, place, pl.ds(0, HALF)]),
        (block_of(below, side), buffer.at[:, place, pl.ds(HALF + TILE, HALF)]),
    ]


def flipped(pairs):
    return [(target, source) for source, target in pairs]


def slot_copies(measured, seen, slot_sems, s):
    return [
        pltpu.make_async_copy(measured.at[s, :, pl.ds(HALF * side, HALF)], seen.at[s, side], slot_sems.at[s, side])
        for side in range(2)
    ]


def fetch_slots(live, centers, wanted, measured, seen, slot_sems, order):
    order[SLOTS_HERE] = 0

    def fetch(s, carry):
        @pl.when(wanted(live[s], centers[s, 0], centers[s, 1]))
        def _():
            for copy in slot_copies(measured, seen, slot_sems, s):
                copy.start()
            count = order[SLOTS_HERE]
            order[count] = s
            order[SLOTS_HERE] = count + 1

        return carry

    lax.fori_loop(0, SLOTS_HERE, fetch, 0)


def run_slots(centers, offset, blocks, measured, seen, slot_sems, order, losses, body):
    def together(first, size):
        chosen = [order[first + i] for i in range(size)]
        for s in chosen:
            wait_all(slot_copies(measured, seen, slot_sems, s))
        runs = []
        for i, s in enumerate(chosen):
            row, column = centers[s, 0] - offset, centers[s, 1] - offset
            block = lax.div(column, HALF)
            runs.append(body(i, s, row, block, jnp.minimum(block + 2, blocks - 1), lax.rem(column, HALF)))
        finished = 0
        while finished < size:
            for s, run in zip(chosen, runs):
                loss = next(run)
                if loss is not None:
                    losses[s] = loss
                    finished += 1

    count = order[SLOTS_HERE]
    pairs = lax.div(count, 2)

    def step(p, carry):
        together(2 * p, 2)
        return carry

    lax.fori_loop(0, pairs, step, 0)

    @pl.when(count > 2 * pairs)
    def _():
        together(count - 1, 1)


def within(row, column):
    return (row >= HALF) & (row <= TILE - HALF) & (column >= HALF) & (column <= TILE - HALF)


def is_inner(alive, row, column):
    return (alive > 0) & within(row, column)


def is_outer(alive, row, column):
    return (alive > 0) & jnp.logical_not(within(row, column))


def inner_kernel(
    centers, live, probe, lefts, rights, pick, field, measured, grad_out, acc, losses, obj, grad, seen, sems, slot_sems, order
):
    slots = [(j, j) for j in range(8)]
    loads = start_all(inner_pairs(field, obj, slots, 0), sems)
    fetch_slots(live, centers, is_inner, measured, seen, slot_sems, order)
    grad[...] = jnp.zeros_like(grad)
    acc[...] = jnp.zeros_like(acc)
    for s in range(SLOTS_HERE):
        losses[s] = 0.0
    wait_all(loads)

    def body(i, s, row, block, block_end, shift):
        return visit(obj, grad, probe, seen, s, lefts, rights, pick, acc, row, block, block_end, shift)

    run_slots(centers, HALF, 8, measured, seen, slot_sems, order, losses, body)
    wait_all(start_all(flipped(inner_pairs(grad_out, grad, slots, 0)), sems))


def outer_kernel(
    centers, live, probe, lefts, rights, pick, field, up, straight, second, measured,
    left, right, above, below, grad_in, acc_in, losses_in,
    grad_out, acc, losses, up_out, down_out, gleft, gright, gabove, gbelow,
    obj, grad, seen, sems, slot_sems, order, grad_sems, down_sems, loaded,
):
    slots = [(j + 1, j) for j in range(8)]
    loads = start_all(
        border_pairs(field, obj, slots)
        + row_pairs(up, 0, obj, slots)
        + strip_pairs(left, above, below, 0, obj, 0)
        + strip_pairs(right, above, below, 1, obj, 9),
        sems,
    )
    relayed = lax.axis_index("gx") == 7
    for chosen, rows in ((relayed, second), (jnp.logical_not(relayed), straight)):
        pl.when(chosen)(functools.partial(start_only, row_pairs(rows, HALF + TILE, obj, slots), down_sems))
    fetch_slots(live, centers, is_outer, measured, seen, slot_sems, order)
    grad_loads = start_all(border_pairs(grad_in, grad, slots), grad_sems)
    for place_at in (0, 9):
        grad[:, place_at] = jnp.zeros((2, ROWS, HALF), jnp.float32)
    for row_at in (0, HALF + TILE):
        grad[:, 1:9, row_at : row_at + HALF] = jnp.zeros((2, 8, HALF, HALF), jnp.float32)
    acc[...] = acc_in[...]
    for s in range(SLOTS_HERE):
        losses[s] = losses_in[s]
    wait_all(loads)
    for i, (source, target) in enumerate(row_pairs(straight, HALF + TILE, obj, slots)):
        pltpu.make_async_copy(source, target, down_sems.at[i]).wait()
    loaded[0] = 0

    def have_grads():
        @pl.when(loaded[0] == 0)
        def _():
            wait_all(grad_loads)
            loaded[0] = 1

    def body(i, s, row, block, block_end, shift):
        return visit(obj, grad, probe, seen, s, lefts, rights, pick, acc, row, block, block_end, shift, None if i else have_grads)

    run_slots(centers, 0, 10, measured, seen, slot_sems, order, losses, body)
    have_grads()
    wait_all(
        start_all(
            flipped(
                strip_pairs(gleft, gabove, gbelow, 0, grad, 0)
                + strip_pairs(gright, gabove, gbelow, 1, grad, 9)
                + band_pairs(up_out, down_out, grad, slots)
                + border_pairs(grad_out, grad, slots)
            ),
            sems,
        )
    )


VMEM_SPEC = pl.BlockSpec(memory_space=pltpu.VMEM)
SMEM_SPEC = pl.BlockSpec(memory_space=pltpu.SMEM)
HBM_SPEC = pl.BlockSpec(memory_space=pl.ANY)


def shaped(*shape):
    return jax.ShapeDtypeStruct(shape, jnp.float32)


def slot_scratch(blocks, copies):
    return [
        pltpu.VMEM((2, blocks, HALF * blocks, HALF), jnp.float32),
        pltpu.VMEM((2, blocks, HALF * blocks, HALF), jnp.float32),
        pltpu.VMEM((SLOTS_HERE, 2, M, HALF), jnp.float32),
        pltpu.SemaphoreType.DMA((copies,)),
        pltpu.SemaphoreType.DMA((SLOTS_HERE, 2)),
        pltpu.SMEM((SLOTS_HERE + 1,), jnp.int32),
    ]


def cost(slots):
    return pl.CostEstimate(flops=slots * 26 * 2 * M**3, bytes_accessed=30 << 20, transcendentals=slots * M * M)


TILE_OUT = (shaped(2, TILE, TILE), shaped(2, 2, M, HALF), shaped(SLOTS_HERE))
TILE_SPECS = (HBM_SPEC, VMEM_SPEC, SMEM_SPEC)


def inner_slots(centers, live, probe, tables, field, measured):
    return pl.pallas_call(
        inner_kernel,
        out_shape=TILE_OUT,
        in_specs=[SMEM_SPEC] * 2 + [VMEM_SPEC] * 4 + [HBM_SPEC] * 2,
        out_specs=TILE_SPECS,
        scratch_shapes=slot_scratch(8, 8),
        compiler_params=pltpu.CompilerParams(vmem_limit_bytes=VMEM),
        cost_estimate=cost(INNER_COST),
        name="inner_slots",
    )(centers, live, probe, *tables, field, measured)


def outer_slots(centers, live, probe, tables, field, up, straight, second, measured, halos, partial):
    return pl.pallas_call(
        outer_kernel,
        out_shape=TILE_OUT + (shaped(2, HALF, TILE),) * 2 + (shaped(2, TILE, HALF),) * 2 + (shaped(2, HALF, 2 * HALF),) * 2,
        in_specs=[SMEM_SPEC] * 2 + [VMEM_SPEC] * 4 + [HBM_SPEC] * 10 + [VMEM_SPEC, SMEM_SPEC],
        out_specs=TILE_SPECS + (HBM_SPEC,) * 6,
        scratch_shapes=slot_scratch(10, 34)
        + [pltpu.SemaphoreType.DMA((12,)), pltpu.SemaphoreType.DMA((8,)), pltpu.SMEM((1,), jnp.int32)],
        input_output_aliases={15: 0},
        compiler_params=pltpu.CompilerParams(vmem_limit_bytes=VMEM),
        cost_estimate=cost(SLOTS_HERE // 2),
        name="outer_slots",
    )(centers, live, probe, *tables, field, up, straight, second, measured, *halos, *partial)


MESH = pl.DeviceIdType.MESH
SHARE = 8
PIECES = CORE // HALF
ROW_PIECES = 4
ROW_STEP = HALF // ROW_PIECES


def return_kernel(
    scale, gleft, gright, gabove, gbelow, gup, gdown, part,
    got_left, got_right, got_up, got_down, out,
    first, second, third, kept1, kept2, kept3, full, edges, from_up, from_down, relay,
    sum_send, sum_recv, strip_send, strip_recv, row_send, row_recv, relay_send, relay_recv, corner_send, corner_recv, local,
):
    gx, gy = lax.axis_index("gx"), lax.axis_index("gy")
    core = lax.rem(gx, 2)
    spot = lax.rem(lax.div(gx, 2), 4)
    upper = lax.div(gx, 8)
    group = upper * 8 + gy
    odd = lax.rem(gy, 2)
    has_up, has_down, has_left, has_right = gx > 0, gx < 15, gy > 0, gy < 7
    crosses = gx == 8
    relays = ((gx == 7) & (odd == 1)) | ((gx == 8) & (odd == 0))
    cross_target = (jnp.where(odd == 0, 7, 8), jnp.where(odd == 0, gy + 1, gy - 1))
    relay_target = (7, jnp.where(gx == 7, gy - 1, gy + 1))
    up, down, left, right = (gx - 1, gy), (gx + 1, gy), (gx, gy - 1), (gx, gy + 1)
    far_pair = (15 - gx, jnp.where(gx == 7, gy - 1, gy + 1))

    def at_spot(k):
        return (gx + 2 * (k - spot), gy)

    def at_group(k):
        return (gx + 8 * (lax.div(k, 8) - upper), lax.rem(k, 8))

    other = (gx + 1 - 2 * core, gy)
    spots = [lax.rem(spot + d, 4) for d in range(1, 4)]
    groups = [lax.rem(group + d, 16) for d in range(1, 16)]
    barrier = pltpu.get_barrier_semaphore()

    def greet(device):
        pl.semaphore_signal(barrier, inc=1, device_id=device, device_id_type=MESH)

    sides = ((has_up, up), (has_down, down), (has_left, left), (has_right, right), (relays, far_pair))
    for there, device in sides:
        pl.when(there)(functools.partial(greet, device))
    always = [other] + [at_spot(k) for k in spots] + [at_group(k) for k in groups]
    for device in always:
        greet(device)
    expected = len(always)
    for there, _ in sides:
        expected = expected + there.astype(jnp.int32)
    pl.semaphore_wait(barrier, expected)

    def remote(source, target, send_sem, recv_sem, device):
        return pltpu.make_async_remote_copy(
            src_ref=source, dst_ref=target, send_sem=send_sem, recv_sem=recv_sem, device_id=device, device_id_type=MESH
        )

    corner_up = remote(gabove, from_down, corner_send.at[0], corner_recv.at[0], up)
    corner_down = remote(gbelow, from_up, corner_send.at[1], corner_recv.at[1], down)
    pl.when(has_up)(corner_up.start)
    pl.when(has_down)(corner_down.start)
    strips = (gleft, gright)
    loads = [
        pltpu.make_async_copy(strips[side].at[:, pl.ds(at, HALF)], edges.at[side, :, pl.ds(to, HALF)], local.at[2 * side + i])
        for side in range(2)
        for i, (at, to) in enumerate(((0, 0), (TILE - HALF, HALF)))
    ]
    for copy in loads:
        copy.start()

    def strip_copy(side, piece):
        if piece < PIECES:
            source = strips[side].at[:, pl.ds(HALF * (piece + 1), HALF)]
            place = HALF * (piece + 1)
        else:
            end = piece - PIECES
            source = edges.at[side, :, pl.ds(HALF * end, HALF)]
            place = (TILE - HALF) * end
        target = (got_right, got_left)[side].at[:, pl.ds(place, HALF)]
        return remote(source, target, strip_send.at[side, piece], strip_recv.at[side, piece], (left, right)[side])

    def strip_start(piece):
        pl.when(has_left)(lambda: strip_copy(0, piece).start())
        pl.when(has_right)(lambda: strip_copy(1, piece).start())

    def strip_sent(piece):
        pl.when(has_left)(lambda: strip_copy(0, piece).wait_send())
        pl.when(has_right)(lambda: strip_copy(1, piece).wait_send())

    def strip_got(piece):
        pl.when(has_right)(lambda: strip_copy(0, piece).wait_recv())
        pl.when(has_left)(lambda: strip_copy(1, piece).wait_recv())

    def row_rows(piece):
        return pl.ds(ROW_STEP * piece, ROW_STEP)

    def row_up(piece, direct):
        source = gup.at[:, row_rows(piece)]
        if direct:
            return remote(source, got_down.at[:, row_rows(piece)], row_send.at[0, piece], row_recv.at[0, piece], up)
        return remote(source, relay.at[:, row_rows(piece)], row_send.at[0, piece], relay_recv.at[piece], cross_target)

    def row_forward(piece):
        return remote(
            relay.at[:, row_rows(piece)], got_down.at[:, row_rows(piece)], relay_send.at[piece], row_recv.at[0, piece], relay_target
        )

    def row_down(piece):
        rows = row_rows(piece)
        return remote(gdown.at[:, rows], got_up.at[:, rows], row_send.at[1, piece], row_recv.at[1, piece], down)

    straight = has_up & (gx != 8)

    def row_start(piece):
        pl.when(straight)(lambda: row_up(piece, True).start())
        pl.when(crosses)(lambda: row_up(piece, False).start())
        pl.when(has_down)(lambda: row_down(piece).start())

    def relay_on(piece):
        def go():
            row_up(piece, False).wait_recv()
            row_forward(piece).start()

        pl.when(relays)(go)

    def rows(start, size):
        return pl.ds(pl.multiple_of(start, 8), size)

    count = [0]

    def send(source, target, device):
        i = count[0]
        count[0] += 1
        copy = remote(source, target, sum_send.at[i], sum_recv.at[i], device)
        copy.start()
        return copy

    def arrive(copies):
        for copy in copies:
            copy.wait_recv()

    strip_start(0)
    stage = [send(part.at[rows((1 - core) * 512, 512)], first, other)]
    sent = list(stage)
    row_start(0)
    strip_start(1)
    arrive(stage)
    kept1[...] = part[rows(core * 512, 512), :] + first[...]
    stage = [send(kept1.at[rows(k * 128, 128)], second.at[d], at_spot(k)) for d, k in enumerate(spots)]
    sent += stage
    for copy in loads:
        copy.wait()

    @pl.when(has_down)
    def _():
        corner_up.wait_recv()
        for side in range(2):
            edges[side, :, HALF:] += from_down[:, :, HALF * side : HALF * (side + 1)]

    @pl.when(has_up)
    def _():
        corner_down.wait_recv()
        for side in range(2):
            edges[side, :, :HALF] += from_up[:, :, HALF * side : HALF * (side + 1)]

    row_start(1)
    strip_start(2)
    strip_sent(0)
    arrive(stage)
    kept2[...] = kept1[rows(spot * 128, 128), :] + (second[0] + second[1] + second[2])
    stage = [send(kept2.at[rows(k * SHARE, SHARE)], third.at[d], at_group(k)) for d, k in enumerate(groups)]
    sent += stage
    relay_on(0)
    row_start(2)
    strip_start(3)
    strip_sent(1)
    arrive(stage)
    total = kept2[rows(group * SHARE, SHARE), :]
    for d in range(15):
        total = total + third[d]
    kept3[...] = total * scale
    mine = rows(core * 512 + spot * 128 + group * SHARE, SHARE)
    full[mine, :] = kept3[...]
    stage = [send(kept3, full.at[mine], at_group(k)) for k in groups]
    sent += stage
    relay_on(1)
    row_start(3)
    strip_start(4)
    strip_sent(2)
    arrive(stage)
    quarter = full.at[rows(core * 512 + spot * 128, 128)]
    stage = [send(quarter, quarter, at_spot(k)) for k in spots]
    sent += stage
    relay_on(2)
    strip_start(5)
    strip_sent(3)
    arrive(stage)
    whole = full.at[rows(core * 512, 512)]
    stage = [send(whole, whole, other)]
    sent += stage
    relay_on(3)
    strip_start(6)
    strip_start(7)
    arrive(stage)
    for part_at in range(2):
        for side in range(2):
            out[part_at, :, HALF * side : HALF * (side + 1)] = full[pl.ds((part_at * 2 + side) * M, M), :]
    for piece in range(4, PIECES + 2):
        strip_sent(piece)
    for piece in range(PIECES + 2):
        strip_got(piece)
    for piece in range(ROW_PIECES):
        pl.when(has_down)(lambda: row_down(piece).wait_send())
        pl.when(has_up)(lambda: row_up(piece, True).wait_send())
        pl.when(relays)(lambda: row_forward(piece).wait_send())
        pl.when(has_down)(lambda: row_up(piece, True).wait_recv())
        pl.when(has_up)(lambda: row_down(piece).wait_recv())
    pl.when(has_up)(corner_up.wait_send)
    pl.when(has_down)(corner_down.wait_send)
    for copy in sent:
        copy.wait_send()


def send_back(gleft, gright, gabove, gbelow, gup, gdown, part, scale):
    copies = 2 * (1 + 3 + 15)
    return pl.pallas_call(
        functools.partial(return_kernel, scale),
        out_shape=(shaped(2, TILE, HALF),) * 2 + (shaped(2, HALF, TILE),) * 2 + (shaped(2, M, M),),
        in_specs=[HBM_SPEC] * 6 + [VMEM_SPEC],
        out_specs=(HBM_SPEC,) * 4 + (VMEM_SPEC,),
        scratch_shapes=[
            pltpu.VMEM((512, HALF), jnp.float32),
            pltpu.VMEM((3, 128, HALF), jnp.float32),
            pltpu.VMEM((15, SHARE, HALF), jnp.float32),
            pltpu.VMEM((512, HALF), jnp.float32),
            pltpu.VMEM((128, HALF), jnp.float32),
            pltpu.VMEM((SHARE, HALF), jnp.float32),
            pltpu.VMEM((1024, HALF), jnp.float32),
            pltpu.VMEM((2, 2, 2 * HALF, HALF), jnp.float32),
            pltpu.VMEM((2, HALF, 2 * HALF), jnp.float32),
            pltpu.VMEM((2, HALF, 2 * HALF), jnp.float32),
            pltpu.VMEM((2, HALF, TILE), jnp.float32),
            pltpu.SemaphoreType.DMA((copies,)),
            pltpu.SemaphoreType.DMA((copies,)),
            pltpu.SemaphoreType.DMA((2, PIECES + 2)),
            pltpu.SemaphoreType.DMA((2, PIECES + 2)),
            pltpu.SemaphoreType.DMA((2, ROW_PIECES)),
            pltpu.SemaphoreType.DMA((2, ROW_PIECES)),
            pltpu.SemaphoreType.DMA((ROW_PIECES,)),
            pltpu.SemaphoreType.DMA((ROW_PIECES,)),
            pltpu.SemaphoreType.DMA((2,)),
            pltpu.SemaphoreType.DMA((2,)),
            pltpu.SemaphoreType.DMA((4,)),
        ],
        compiler_params=pltpu.CompilerParams(collective_id=0, has_side_effects=True, vmem_limit_bytes=VMEM),
        cost_estimate=pl.CostEstimate(flops=M * M * 8, bytes_accessed=100 << 20, transcendentals=0),
        name="send_back",
    )(gleft, gright, gabove, gbelow, gup, gdown, part.reshape(1024, HALF))


def fold_kernel(got_left, got_right, got_up, got_down, tile, out, band, side_band, row_in, strip_in, sems, out_sems):
    gx, gy = lax.axis_index("gx"), lax.axis_index("gy")
    end = TILE - HALF
    frame = [
        (tile.at[:, pl.ds(0, HALF)], band.at[0]),
        (tile.at[:, pl.ds(end, HALF)], band.at[1]),
        (tile.at[:, pl.ds(HALF, CORE), pl.ds(0, HALF)], side_band.at[0]),
        (tile.at[:, pl.ds(HALF, CORE), pl.ds(end, HALF)], side_band.at[1]),
    ]
    arrived = [(got_up, row_in.at[0]), (got_down, row_in.at[1]), (got_left, strip_in.at[0]), (got_right, strip_in.at[1])]
    loads = start_all(frame + arrived, sems)
    below, right = gx < 15, gy < 7
    above, left = gx > 0, gy > 0

    def add_strip(i, there, target, rows):
        @pl.when(there)
        def _():
            target[...] += strip_in[i, :, rows]

    def write(i, source, target):
        copy = pltpu.make_async_copy(source, target, out_sems.at[i])
        copy.start()
        return copy

    stores = []
    for i, there in enumerate((left, right)):
        loads[2 + i].wait()
        loads[6 + i].wait()
        add_strip(i, there, side_band.at[i], slice(HALF, end))
        stores.append(write(i, side_band.at[i], out.at[:, pl.ds(HALF, CORE), pl.ds(end * i, HALF)]))
    for i, there in enumerate((above, below)):
        loads[i].wait()
        loads[4 + i].wait()

        @pl.when(there)
        def _():
            band[i] += row_in[i]

        for j, beside in enumerate((left, right)):
            add_strip(j, beside, band.at[i, :, :, pl.ds(end * j, HALF)], slice(end * i, end * i + HALF))
        stores.append(write(2 + i, band.at[i], out.at[:, pl.ds(end * i, HALF)]))
    wait_all(stores)


def fold(tile, got_left, got_right, got_up, got_down):
    return pl.pallas_call(
        fold_kernel,
        out_shape=shaped(2, TILE, TILE),
        in_specs=[HBM_SPEC] * 5,
        out_specs=HBM_SPEC,
        scratch_shapes=[
            pltpu.VMEM((2, 2, HALF, TILE), jnp.float32),
            pltpu.VMEM((2, 2, CORE, HALF), jnp.float32),
            pltpu.VMEM((2, 2, HALF, TILE), jnp.float32),
            pltpu.VMEM((2, 2, TILE, HALF), jnp.float32),
            pltpu.SemaphoreType.DMA((8,)),
            pltpu.SemaphoreType.DMA((4,)),
        ],
        input_output_aliases={4: 0},
        compiler_params=pltpu.CompilerParams(vmem_limit_bytes=VMEM),
        name="fold",
    )(got_left, got_right, got_up, got_down, tile)


def shift_by_one(x, axis, forward):
    count = lax.axis_size(axis)
    steps = [(i, i + 1) if forward else (i + 1, i) for i in range(count - 1)]
    return lax.ppermute(x, axis, steps)


def to_right(x):
    return shift_by_one(x, "gy", True)


def to_left(x):
    return shift_by_one(x, "gy", False)


def to_down(x):
    return shift_by_one(x, "gx", True)


def to_up(x):
    return shift_by_one(x, "gx", False)


def joint(x, pairs):
    return lax.ppermute(x, ("gx", "gy"), [(8 * a + b, 8 * c + d) for (a, b), (c, d) in pairs])


def crossing_first(x):
    return joint(
        x, [((8, 2 * y), (7, 2 * y + 1)) for y in range(4)] + [((8, 2 * y + 1), (8, 2 * y)) for y in range(4)]
    )


def crossing_second(x):
    return joint(x, [((7, 2 * y + 1), (7, 2 * y)) for y in range(4)] + [((8, 2 * y), (7, 2 * y + 1)) for y in range(4)])


def to_up_straight(x):
    return lax.ppermute(x, "gx", [(i + 1, i) for i in range(15) if i != 7])


def on_device(field, probe, centers, live, measured):
    tables = tuple(jnp.asarray(t) for t in host_tables())
    last, first, later = lax.optimization_barrier((field[:, :, TILE - HALF :], field[:, :, :HALF], field))
    left, right = to_right(last), to_left(first)
    top_rows = later[:, :HALF]
    relayed, up, straight = crossing_first(top_rows), to_down(later[:, TILE - HALF :]), to_up_straight(top_rows)
    grad, acc, losses = inner_slots(centers, live, probe, tables, field, measured)
    relayed, acc = lax.optimization_barrier((relayed, acc))
    second = crossing_second(relayed)
    left, right, up, straight, acc = lax.optimization_barrier((left, right, up, straight, acc))
    above = to_down(jnp.concatenate([left[:, TILE - HALF :], right[:, TILE - HALF :]], axis=2))
    below = to_up(jnp.concatenate([left[:, :HALF], right[:, :HALF]], axis=2))
    halos = (left, right, above, below)
    partial = (grad, acc, losses)
    grad, acc, losses, gup, gdown, gleft, gright, gabove, gbelow = outer_slots(
        centers, live, probe, tables, field, up, straight, second, measured, halos, partial
    )
    slots_all = SLOTS_HERE * lax.axis_size("gx") * lax.axis_size("gy")
    *got, probe_grad = send_back(gleft, gright, gabove, gbelow, gup, gdown, acc, 1.0 / math.sqrt(slots_all))
    return fold(grad, *got), probe_grad, losses


def solution(mesh):
    placed = (
        P(None, "gx", "gy"),
        P(),
        P(("gx", "gy"), None),
        P(("gx", "gy")),
        P(("gx", "gy"), None, None),
    )
    return jax.shard_map(
        on_device,
        mesh=mesh,
        in_specs=placed,
        out_specs=(P(None, "gx", "gy"), P(), P(("gx", "gy"))),
        check_vma=False,
    )
```
